128 devices in a mesh: tok: 4 (over y_hi, core), wt: 32 (over x, z, y_lo).
Axes of the slice: x: 4, y: 4 (y_hi: 2, y_lo: 2; y = y_hi * 2 + y_lo), z: 4, core: 2. Of those that a mesh axis runs over, the one named last changes fastest.
Arguments:
- activations: bfloat16 [1536, 8192], P('tok', 'wt'), may hold values from -6 to 6
- gate_pre: bfloat16 [1536, 16384], P('tok', 'wt'), may hold values from -6 to 6
- up_pre: bfloat16 [1536, 16384], P('tok', 'wt'), may hold values from -6 to 6
- hidden_grad: bfloat16 [1536, 16384], P('tok', 'wt'), may hold values from -0.59765625 to 0.59765625
- gate_blocks: bfloat16 [4096, 128, 128], P('wt'), may hold values from -0.125 to 0.125
- up_blocks: bfloat16 [4096, 128, 128], P('wt'), may hold values from -0.125 to 0.125
- block_rows: int32 [4096], P('wt'), may hold values from 0 to 127, as said below
- block_cols: int32 [4096], P('wt'), may hold values from 0 to 63, as said below
- block_count: int32 [32], P('wt'), may hold values from 32 to 128, as said below
Outputs:
- input_grad: bfloat16 [1536, 8192], P('tok', 'wt')
- gate_weight_grad: bfloat16 [4096, 128, 128], P('wt')
- up_weight_grad: bfloat16 [4096, 128, 128], P('wt')
The draws below stay inside these ranges and needn't reach their ends.
Inputs may be any that keep to these rules, and one draw needn't show every extreme that they name: `block_rows`: slots of wt index w are w * 128 to (w + 1) * 128 - 1; their block rows lie in w * 4 to (w + 1) * 4 - 1; slots past the count repeat the owner's first slot. `block_cols`: the live slots of one owner name distinct blocks. `block_count`: one owner holds exactly 128 kept blocks.
All inputs are finite; a program needn't handle non-finite values.
Results may differ from the reference program's by a relative error of at most 0.025.
Values may be sent and summed in bfloat16 or wider, within the bound.
No kernel may reach another device: no remote copies, remote signals or barrier semaphores. Data moves between devices by JAX's collectives and lax.ppermute only.
A program may use at most 192 MiB of HBM per device.

```python
import jax
import jax.numpy as jnp
from jax import lax

D = 8192
FF = 16384
BLK = 128
TOK_DEV = 384
TOKENS = 1536
DBLK = 64
FBLK = 128
ROWS_DEV = 4
KEEP = 64
MAXB = 128
N_TOK = 4
N_WT = 32


def pattern(key):
    counts = jax.random.randint(jax.random.fold_in(key, 1), (N_WT,), KEEP // 2, 3 * KEEP // 2 + 1)
    heavy = jax.random.randint(jax.random.fold_in(key, 2), (), 0, N_WT)
    counts = jnp.where(jnp.arange(N_WT) == heavy, MAXB, counts).astype(jnp.int32)
    pairs = ROWS_DEV * DBLK
    scores = jax.random.randint(jax.random.fold_in(key, 3), (N_WT, pairs), 0, 1024) * pairs + jnp.arange(pairs)[None, :]
    order = jnp.argsort(scores, axis=1)[:, :MAXB]
    slot_index = jnp.arange(MAXB)[None, :]
    chosen = jnp.where(slot_index < counts[:, None], order, order[:, :1])
    rows = jnp.arange(N_WT)[:, None] * ROWS_DEV + chosen // DBLK
    cols = chosen % DBLK
    return (counts, rows.reshape(-1).astype(jnp.int32), cols.reshape(-1).astype(jnp.int32))


def draw_block_rows(key, part):
    shared = pattern(key)
    return shared[1]


def draw_block_cols(key, part):
    shared = pattern(key)
    return shared[2]


def draw_block_count(key, part):
    shared = pattern(key)
    return shared[0]


def shard_levels(own_key, shape, cuts, least, high):
    def one(position, parts):
        steps = jax.random.uniform(jax.random.fold_in(jax.random.fold_in(own_key, 6), position), (parts,), jnp.float32, least / len(cuts), high / len(cuts))
        return jnp.repeat(jnp.exp(steps), shape[position] // parts).reshape((-1,) + (1,) * (len(shape) - position - 1))

    gain = one(*cuts[0])
    for cut in cuts[1:]:
        gain = gain * one(*cut)
    return gain


def gaussian(key, dims, deviation, reach, split=(), kind=jnp.bfloat16):
    entries = deviation * jax.random.normal(key, dims, jnp.float32)
    if split:
        entries = entries * shard_levels(key, dims, split, -0.22, 0.18)
    return jnp.clip(entries, -reach, reach).astype(kind)


def setup_inputs(seed: int = 0) -> dict:
    arg_keys = jax.random.split(jax.random.key(seed), 10)
    activations = gaussian(arg_keys[0], (TOKENS, D), 1.0, 6.0, ((0, 4), (1, 32)))
    gate_pre = gaussian(arg_keys[1], (TOKENS, FF), 1.5, 6.0, ((0, 4), (1, 32)))
    up_pre = gaussian(arg_keys[2], (TOKENS, FF), 1.0, 6.0, ((0, 4), (1, 32)))
    hidden_grad = gaussian(arg_keys[3], (TOKENS, FF), 0.1, 0.59765625, ((0, 4), (1, 32)))
    gate_blocks = gaussian(arg_keys[4], (N_WT * MAXB, BLK, BLK), (D // 4) ** -0.5, 0.125, ((0, 32),))
    up_blocks = gaussian(arg_keys[5], (N_WT * MAXB, BLK, BLK), (D // 4) ** -0.5, 0.125, ((0, 32),))
    block_rows = draw_block_rows(jax.random.fold_in(arg_keys[9], 71), 0)
    block_cols = draw_block_cols(jax.random.fold_in(arg_keys[9], 71), 0)
    block_count = draw_block_count(jax.random.fold_in(arg_keys[9], 71), 0)
    return dict(activations=activations, gate_pre=gate_pre, up_pre=up_pre, hidden_grad=hidden_grad, gate_blocks=gate_blocks, up_blocks=up_blocks, block_rows=block_rows, block_cols=block_cols, block_count=block_count)


def reference(activations, gate_pre, up_pre, hidden_grad, gate_blocks, up_blocks, block_rows, block_cols, block_count):
    gate_value = gate_pre.astype(jnp.float32)
    up_value = up_pre.astype(jnp.float32)
    grad_value = hidden_grad.astype(jnp.float32)
    sigmoid_gate = jax.nn.sigmoid(gate_value)
    gate_grad = (grad_value * up_value * sigmoid_gate * (1.0 + gate_value * (1.0 - sigmoid_gate))).astype(jnp.bfloat16)
    up_grad = (grad_value * gate_value * sigmoid_gate).astype(jnp.bfloat16)
    token_count = activations.shape[0]
    gate_cols = gate_grad.reshape(token_count, FBLK, BLK)
    up_cols = up_grad.reshape(token_count, FBLK, BLK)
    feature_cols = activations.reshape(token_count, DBLK, BLK)
    slot_index = jnp.arange(N_WT * MAXB, dtype=jnp.int32) % MAXB
    alive = (slot_index < jnp.repeat(block_count, MAXB)).reshape(N_WT, MAXB)
    rows = block_rows.reshape(N_WT, MAXB)
    cols = block_cols.reshape(N_WT, MAXB)
    gate_w = gate_blocks.reshape(N_WT, MAXB, BLK, BLK)
    up_w = up_blocks.reshape(N_WT, MAXB, BLK, BLK)

    def owner(carry, inputs):
        rows_w, cols_w, alive_w, gate_ww, up_ww = inputs
        mask = alive_w[:, None, None]
        gate_m = jnp.where(mask, gate_ww.astype(jnp.float32), jnp.float32(0.0))
        up_m = jnp.where(mask, up_ww.astype(jnp.float32), jnp.float32(0.0))
        gate_sel = jnp.take(gate_cols, rows_w, axis=1).astype(jnp.float32)
        up_sel = jnp.take(up_cols, rows_w, axis=1).astype(jnp.float32)
        contrib = jnp.einsum('tsj,sjk->tsk', gate_sel, gate_m) + jnp.einsum('tsj,sjk->tsk', up_sel, up_m)
        summed = jax.ops.segment_sum(jnp.transpose(contrib, (1, 0, 2)), cols_w, num_segments=DBLK)
        feature_sel = jnp.take(feature_cols, cols_w, axis=1).astype(jnp.float32)
        results = []
        for chosen in (gate_sel, up_sel):
            total = jnp.zeros((MAXB, BLK, BLK), jnp.float32)
            for group in range(N_TOK):
                lower = group * TOK_DEV
                upper = lower + TOK_DEV
                partial_sum = jnp.einsum('tsj,tsk->sjk', chosen[lower:upper], feature_sel[lower:upper])
                rounded = lax.optimization_barrier(partial_sum.astype(jnp.bfloat16))
                total = total + rounded.astype(jnp.float32)
            results.append(jnp.where(mask, total, jnp.float32(0.0)).astype(jnp.bfloat16))
        return carry + summed, (results[0], results[1])

    start = jnp.zeros((DBLK, token_count, BLK), jnp.float32)
    total_grad, grads = lax.scan(owner, start, (rows, cols, alive, gate_w, up_w))
    input_grad = jnp.transpose(total_grad, (1, 0, 2)).reshape(token_count, DBLK * BLK).astype(jnp.bfloat16)
    gate_weight_grad = grads[0].reshape(N_WT * MAXB, BLK, BLK)
    up_weight_grad = grads[1].reshape(N_WT * MAXB, BLK, BLK)
    return (input_grad, gate_weight_grad, up_weight_grad)
```

```python
import functools

import jax
import jax.numpy as jnp
from jax import lax
from jax.experimental import pallas as pl
from jax.experimental.pallas import tpu as pltpu
from jax.sharding import Mesh
from jax.sharding import PartitionSpec as P

BF = jnp.bfloat16
F32 = jnp.float32
AXES = {"x": ("c", "x"), "z": ("c", "z"), "y": ("yh", "c", "yl")}
SIZES = {"yh": 2, "c": 2, "x": 4, "z": 4, "yl": 2}
TOK = 384
SLOTS = 128
HALF = 64
PAIRS = 36


def shift(value, axis, step):
    pairs = []
    if axis in ("yh", "c", "yl"):
        return lax.ppermute(value, axis, [(0, 1), (1, 0)])
    if axis == "y":
        for yh in range(2):
            for c in range(2):
                for yl in range(2):
                    y = (yh * 2 + yl + (step if c == 0 else -step)) % 4
                    pairs.append(((yh * 2 + c) * 2 + yl, ((y // 2) * 2 + c) * 2 + y % 2))
    else:
        for c in range(2):
            for a in range(4):
                b = (a + (step if c == 0 else -step)) % 4
                pairs.append((c * 4 + a, c * 4 + b))
    return lax.ppermute(value, AXES[axis], pairs)


def add(a, b):
    return (a.astype(F32) + b.astype(F32)).astype(BF)


def terms_kernel(
    tab, order, gate_ref, up_ref, hid_ref, wg_hbm, wu_hbm,
    gut_ref, t0_hbm, t1_hbm, t2_hbm, t3_hbm,
    wbuf, gu, tbuf, wsem, tsem,
):
    copies = [
        pltpu.make_async_copy(wg_hbm, wbuf.at[pl.ds(0, SLOTS), pl.ds(0, 128), :], wsem.at[0]),
        pltpu.make_async_copy(wu_hbm, wbuf.at[pl.ds(0, SLOTS), pl.ds(128, 128), :], wsem.at[1]),
    ]
    for copy in copies:
        copy.start()
    wbuf[SLOTS] = jnp.zeros((256, 128), BF)
    for r in range(4):
        cols = pl.ds(r * 128, 128)
        g = gate_ref[:, cols].astype(F32)
        u = up_ref[:, cols].astype(F32)
        h = hid_ref[:, cols].astype(F32)
        sig = 1.0 / (1.0 + jnp.exp(-g))
        gg = h * u * sig * (1.0 + g * (1.0 - sig))
        ug = h * g * sig
        gu[:, pl.ds(r * 256, 128)] = gg.astype(BF)
        gu[:, pl.ds(r * 256 + 128, 128)] = ug.astype(BF)
        gut_ref[pl.ds(r * 256, 128), :] = gg.T.astype(BF)
        gut_ref[pl.ds(r * 256 + 128, 128), :] = ug.T.astype(BF)
    for copy in copies:
        copy.wait()
    outs = []
    for n, (k, dst) in enumerate(((1, t1_hbm), (2, t2_hbm), (3, t3_hbm), (0, t0_hbm))):

        @pl.loop(0, 8)
        def _(j):
            base = order[k * 8 + j]
            total = jnp.zeros((TOK, 256), F32)
            for r in range(4):
                left = wbuf[tab[r * 64 + base]]
                right = wbuf[tab[r * 64 + base + 1]]
                both = jnp.concatenate([left, right], axis=1)
                total += jnp.dot(gu[:, r * 256 : (r + 1) * 256], both, preferred_element_type=F32)
            tbuf[k * 8 + j] = total.astype(BF)

        out = pltpu.make_async_copy(tbuf.at[pl.ds(k * 8, 8)], dst, tsem.at[n])
        out.start()
        outs.append(out)
    for out in outs:
        out.wait()


def terms(tab, order, gate_pre, up_pre, hidden, wg, wu):
    piece = jax.ShapeDtypeStruct((8, TOK, 256), BF)
    vm = pl.BlockSpec(memory_space=pltpu.VMEM)
    anyspace = pl.BlockSpec(memory_space=pl.ANY)
    return pl.pallas_call(
        terms_kernel,
        out_shape=[jax.ShapeDtypeStruct((1024, TOK), BF)] + [piece] * 4,
        in_specs=[pl.BlockSpec(memory_space=pltpu.SMEM)] * 2 + [vm] * 3 + [anyspace] * 2,
        out_specs=[vm] + [anyspace] * 4,
        scratch_shapes=[
            pltpu.VMEM((SLOTS + 1, 256, 128), BF),
            pltpu.VMEM((TOK, 1024), BF),
            pltpu.VMEM((32, TOK, 256), BF),
            pltpu.SemaphoreType.DMA((2,)),
            pltpu.SemaphoreType.DMA((4,)),
        ],
        compiler_params=pltpu.CompilerParams(vmem_limit_bytes=40 * 1024 * 1024),
        cost_estimate=pl.CostEstimate(flops=2 * TOK * 1024 * 8192, bytes_accessed=18 << 20, transcendentals=TOK * 512),
        name="terms",
    )(tab, order, gate_pre, up_pre, hidden, wg, wu)


def wgrad_kernel(
    lrow, lslot, lact, meta, own_ref, other_ref, *rest,
):
    pieces, out_hbm = rest[:8], rest[8]
    acts, gt, stage, asem, osem = rest[9:]
    copies = [
        pltpu.make_async_copy(piece, acts.at[pl.ds(n * 16, 16)], asem.at[n]) for n, piece in enumerate(pieces)
    ]
    for copy in copies:
        copy.start()
    gt[:, :TOK] = own_ref[...]
    gt[:, TOK:] = other_ref[...]

    @pl.loop(meta[2], SLOTS)
    def _(s):
        stage[s] = jnp.zeros((256, 128), BF)

    for copy in copies:
        copy.wait()
    outs = []
    for h in range(2):

        @pl.loop(0, meta[h])
        def _(p):
            pos = (h * PAIRS + p) * 2
            rows = pl.ds(pl.multiple_of(lrow[pos] * 256, 256), 256)
            left = jnp.concatenate([acts[lact[pos * 2]], acts[lact[pos * 2 + 1]]], axis=0)
            right = jnp.concatenate([acts[lact[pos * 2 + 2]], acts[lact[pos * 2 + 3]]], axis=0)
            both = jnp.concatenate([left, right], axis=1)
            total = jnp.dot(gt[rows, :], both, preferred_element_type=F32).astype(BF)
            stage[lslot[pos]] = total[:, :128]
            stage[lslot[pos + 1]] = total[:, 128:]

        out = pltpu.make_async_copy(
            stage.at[pl.ds(h * HALF, HALF)], out_hbm.at[pl.ds(h * HALF, HALF)], osem.at[h]
        )
        out.start()
        outs.append(out)
    for out in outs:
        out.wait()


def wgrad(lrow, lslot, lact, meta, own, other, pieces):
    vm = pl.BlockSpec(memory_space=pltpu.VMEM)
    anyspace = pl.BlockSpec(memory_space=pl.ANY)
    return pl.pallas_call(
        wgrad_kernel,
        out_shape=jax.ShapeDtypeStruct((SLOTS, 256, 128), BF),
        in_specs=[pl.BlockSpec(memory_space=pltpu.SMEM)] * 4 + [vm] * 2 + [anyspace] * 8,
        out_specs=anyspace,
        scratch_shapes=[
            pltpu.VMEM((128, TOK, 128), BF),
            pltpu.VMEM((1024, 2 * TOK), BF),
            pltpu.VMEM((SLOTS + 1, 256, 128), BF),
            pltpu.SemaphoreType.DMA((8,)),
            pltpu.SemaphoreType.DMA((2,)),
        ],
        compiler_params=pltpu.CompilerParams(vmem_limit_bytes=40 * 1024 * 1024),
        cost_estimate=pl.CostEstimate(flops=2 * 768 * 256 * 128 * 128, bytes_accessed=22 << 20, transcendentals=0),
        name="wgrad",
    )(lrow, lslot, lact, meta, own, other, *pieces)


def tables(block_rows, block_cols, block_count):
    i32 = jnp.int32
    c = lax.axis_index("c")
    x, z = lax.axis_index("x"), lax.axis_index("z")
    yh, yl = lax.axis_index("yh"), lax.axis_index("yl")
    sign = 1 - 2 * c
    slots = jnp.arange(SLOTS, dtype=i32)
    live = slots < block_count[0]
    row = block_rows % 4
    col = block_cols
    key = jnp.where(live, row * 64 + col, -1)
    hit = key[None, :] == jnp.arange(256, dtype=i32)[:, None]
    tab = jnp.min(jnp.where(hit, slots[None, :], SLOTS), axis=1)
    k = jnp.arange(4, dtype=i32)
    xs = (x - sign * k) % 4
    zs = (z - sign * k) % 4
    ys = yl ^ jnp.arange(2, dtype=i32)
    order = (((xs[:, None, None] * 4 + zs[None, :, None]) * 2 + ys[None, None, :]) * 2).reshape(32)
    half = slots // HALF
    same = (row[:, None] == row[None, :]) & (half[:, None] == half[None, :]) & live[None, :]
    rank = jnp.sum(jnp.where(same & (slots[None, :] < slots[:, None]), 1, 0), axis=1)
    count = jnp.sum(
        jnp.where(
            live[None, None, :]
            & (half[None, None, :] == jnp.arange(2, dtype=i32)[:, None, None])
            & (row[None, None, :] == k[None, :, None]),
            1,
            0,
        ),
        axis=2,
    )
    npair = (count + 1) // 2
    first = jnp.sum(jnp.where(k[None, :, None] > k[None, None, :], npair[:, None, :], 0), axis=2)
    mine = (jnp.arange(2, dtype=i32)[None, :, None] == half[:, None, None]) & (
        k[None, None, :] == row[:, None, None]
    )
    start = jnp.sum(jnp.where(mine, first[None], 0), axis=(1, 2))
    place = jnp.where(live, (half * PAIRS + start) * 2 + rank, -1)
    spots = jnp.arange(4 * PAIRS, dtype=i32)
    at = place[None, :] == spots[:, None]
    lslot = jnp.min(jnp.where(at, slots[None, :], SLOTS), axis=1)
    lrow = jnp.sum(jnp.where(at, row[None, :], 0), axis=1)
    lcol = jnp.sum(jnp.where(at, col[None, :], 0), axis=1)
    cx, cz, cy, par = lcol >> 4, (lcol >> 2) & 3, (lcol >> 1) & 1, lcol & 1
    kx = (sign * (x - cx)) % 4
    kz = (sign * (z - cz)) % 4
    lact = []
    for j in range(2):
        ky = (sign * ((yh * 2 + yl) - ((yh ^ j) * 2 + cy))) % 4
        lact.append(jnp.where(par == 0, ky * 16 + kz * 4 + kx, 64 + kz * 16 + ky * 4 + kx))
    lact = jnp.stack(lact, axis=1).reshape(-1)
    meta = jnp.concatenate([jnp.sum(npair, axis=1), block_count]).astype(i32)
    return tab, order, lrow, lslot, lact, meta


def gather_direct(value, axis):
    return [value] + [shift(value, axis, k) for k in (1, 2, 3)]


def gather_ring(value, axis):
    parts = [value]
    for _ in range(3):
        parts.append(shift(parts[-1], axis, 1))
    return parts


def body(
    activations, gate_pre, up_pre, hidden_grad, gate_blocks, up_blocks, block_rows, block_cols, block_count,
):
    tab, order, lrow, lslot, lact, meta = tables(block_rows, block_cols, block_count)
    both = jnp.stack([activations[:, :128], activations[:, 128:]])
    near = gather_direct(both, "x")
    even = jnp.stack([v[0] for v in near])
    odd = jnp.stack([v[1] for v in near])
    gut, t0, t1, t2, t3 = terms(tab, order, gate_pre, up_pre, hidden_grad, gate_blocks, up_blocks)
    other = shift(gut, "yh", 1)
    even = jnp.concatenate(gather_direct(even, "z"))
    odd = jnp.concatenate(gather_direct(odd, "y"))
    pieces = gather_ring(even, "y") + gather_ring(odd, "z")
    moving = shift(t1, "x", 1)
    moving = shift(add(moving, t2), "x", 1)
    moving = shift(add(moving, t3), "x", 1)
    mine = add(moving, t0).reshape(4, 2, TOK, 256)
    moving = shift(mine[1], "z", 1)
    moving = shift(add(moving, mine[2]), "z", 1)
    moving = shift(add(moving, mine[3]), "z", 1)
    keep = moving[0].astype(F32) + mine[0, 0].astype(F32)
    send = add(moving[1], mine[0, 1])
    input_grad = (keep + shift(send, "yl", 1).astype(F32)).astype(BF)
    part = wgrad(lrow, lslot, lact, meta, gut, other, pieces)
    total = add(part, shift(part, "c", 1))
    return input_grad, total[:, :128], total[:, 128:]


def solution(mesh):
    fine = Mesh(mesh.devices.reshape(2, 2, 4, 4, 2), ("yh", "c", "x", "z", "yl"))
    tok, wt = ("yh", "c"), ("x", "z", "yl")
    in_specs = (P(tok, wt),) * 4 + (P(wt, None, None),) * 2 + (P(wt),) * 3
    out_specs = (P(tok, wt), P(wt, None, None), P(wt, None, None))
    return jax.shard_map(body, mesh=fine, in_specs=in_specs, out_specs=out_specs, check_vma=False)
```

```python
import functools

import jax
import jax.numpy as jnp
from jax import lax
from jax.experimental import pallas as pl
from jax.experimental.pallas import tpu as pltpu
from jax.sharding import Mesh
from jax.sharding import PartitionSpec as P

BF = jnp.bfloat16
F32 = jnp.float32
AXES = {"x": ("c", "x"), "z": ("c", "z"), "y": ("yh", "c", "yl")}
SIZES = {"yh": 2, "c": 2, "x": 4, "z": 4, "yl": 2}
TOK = 384
SLOTS = 128
HALF = 64
PAIRS = 36


def shift(value, axis, step):
    pairs = []
    if axis in ("yh", "c", "yl"):
        return lax.ppermute(value, axis, [(0, 1), (1, 0)])
    if axis == "y":
        for yh in range(2):
            for c in range(2):
                for yl in range(2):
                    y = (yh * 2 + yl + (step if c == 0 else -step)) % 4
                    pairs.append(((yh * 2 + c) * 2 + yl, ((y // 2) * 2 + c) * 2 + y % 2))
    else:
        for c in range(2):
            for a in range(4):
                b = (a + (step if c == 0 else -step)) % 4
                pairs.append((c * 4 + a, c * 4 + b))
    return lax.ppermute(value, AXES[axis], pairs)


def add(a, b):
    return (a.astype(F32) + b.astype(F32)).astype(BF)


def load_blocks(wg_hbm, wu_hbm, wbuf, wsem):
    copies = [
        pltpu.make_async_copy(wg_hbm, wbuf.at[pl.ds(0, SLOTS), pl.ds(0, 128), :], wsem.at[0]),
        pltpu.make_async_copy(wu_hbm, wbuf.at[pl.ds(0, SLOTS), pl.ds(128, 128), :], wsem.at[1]),
    ]
    for copy in copies:
        copy.start()
    wbuf[SLOTS] = jnp.zeros((256, 128), BF)
    return copies


def term_chunk(k, tab, order, gu, wbuf, out):
    @pl.loop(0, 8)
    def _(j):
        base = order[k * 8 + j]
        total = jnp.zeros((TOK, 256), F32)
        for r in range(4):
            left = wbuf[tab[r * 64 + base]]
            right = wbuf[tab[r * 64 + base + 1]]
            both = jnp.concatenate([left, right], axis=1)
            total += jnp.dot(gu[:, r * 256 : (r + 1) * 256], both, preferred_element_type=F32)
        out[j] = total.astype(BF)


def first_kernel(tab, order, gate_ref, up_ref, hid_ref, wg_hbm, wu_hbm, gu, gut_ref, t1, wbuf, wsem):
    copies = load_blocks(wg_hbm, wu_hbm, wbuf, wsem)
    for r in range(4):
        cols = pl.ds(r * 128, 128)
        g = gate_ref[:, cols].astype(F32)
        u = up_ref[:, cols].astype(F32)
        h = hid_ref[:, cols].astype(F32)
        sig = 1.0 / (1.0 + jnp.exp(-g))
        gg = h * u * sig * (1.0 + g * (1.0 - sig))
        ug = h * g * sig
        gu[:, pl.ds(r * 256, 128)] = gg.astype(BF)
        gu[:, pl.ds(r * 256 + 128, 128)] = ug.astype(BF)
        gut_ref[pl.ds(r * 256, 128), :] = gg.T.astype(BF)
        gut_ref[pl.ds(r * 256 + 128, 128), :] = ug.T.astype(BF)
    for copy in copies:
        copy.wait()
    term_chunk(1, tab, order, gu, wbuf, t1)


def rest_kernel(tab, order, gu, wg_hbm, wu_hbm, t2, t3, t0, wbuf, wsem):
    for copy in load_blocks(wg_hbm, wu_hbm, wbuf, wsem):
        copy.wait()
    for k, out in ((2, t2), (3, t3), (0, t0)):
        term_chunk(k, tab, order, gu, wbuf, out)


PIECE = jax.ShapeDtypeStruct((8, TOK, 256), BF)
VM = pl.BlockSpec(memory_space=pltpu.VMEM)
SM = pl.BlockSpec(memory_space=pltpu.SMEM)
ANY = pl.BlockSpec(memory_space=pl.ANY)
BLOCK_SCRATCH = [pltpu.VMEM((SLOTS + 1, 256, 128), BF), pltpu.SemaphoreType.DMA((2,))]


def first_terms(tab, order, gate_pre, up_pre, hidden, wg, wu):
    return pl.pallas_call(
        first_kernel,
        out_shape=[jax.ShapeDtypeStruct((TOK, 1024), BF), jax.ShapeDtypeStruct((1024, TOK), BF), PIECE],
        in_specs=[SM] * 2 + [VM] * 3 + [ANY] * 2,
        out_specs=[VM] * 3,
        scratch_shapes=BLOCK_SCRATCH,
        compiler_params=pltpu.CompilerParams(vmem_limit_bytes=40 * 1024 * 1024),
        cost_estimate=pl.CostEstimate(flops=2 * TOK * 1024 * 2048, bytes_accessed=14 << 20, transcendentals=TOK * 512),
        name="first_terms",
    )(tab, order, gate_pre, up_pre, hidden, wg, wu)


def rest_terms(tab, order, gu, wg, wu):
    return pl.pallas_call(
        rest_kernel,
        out_shape=[PIECE] * 3,
        in_specs=[SM] * 2 + [VM] + [ANY] * 2,
        out_specs=[VM] * 3,
        scratch_shapes=BLOCK_SCRATCH,
        compiler_params=pltpu.CompilerParams(vmem_limit_bytes=40 * 1024 * 1024),
        cost_estimate=pl.CostEstimate(flops=2 * TOK * 1024 * 6144, bytes_accessed=16 << 20, transcendentals=0),
        name="rest_terms",
    )(tab, order, gu, wg, wu)


def wgrad_kernel(
    lrow, lslot, lact, meta, own_ref, other_ref, *rest,
):
    pieces, out_hbm = rest[:8], rest[8]
    acts, gt, stage, asem, osem = rest[9:]
    copies = [
        pltpu.make_async_copy(piece, acts.at[pl.ds(n * 16, 16)], asem.at[n]) for n, piece in enumerate(pieces)
    ]
    for copy in copies:
        copy.start()
    gt[:, :TOK] = own_ref[...]
    gt[:, TOK:] = other_ref[...]

    @pl.loop(meta[2], SLOTS)
    def _(s):
        stage[s] = jnp.zeros((256, 128), BF)

    for copy in copies:
        copy.wait()
    outs = []
    for h in range(2):

        @pl.loop(0, meta[h])
        def _(p):
            pos = (h * PAIRS + p) * 2
            rows = pl.ds(pl.multiple_of(lrow[pos] * 256, 256), 256)
            left = jnp.concatenate([acts[lact[pos * 2]], acts[lact[pos * 2 + 1]]], axis=0)
            right = jnp.concatenate([acts[lact[pos * 2 + 2]], acts[lact[pos * 2 + 3]]], axis=0)
            both = jnp.concatenate([left, right], axis=1)
            total = jnp.dot(gt[rows, :], both, preferred_element_type=F32).astype(BF)
            stage[lslot[pos]] = total[:, :128]
            stage[lslot[pos + 1]] = total[:, 128:]

        out = pltpu.make_async_copy(
            stage.at[pl.ds(h * HALF, HALF)], out_hbm.at[pl.ds(h * HALF, HALF)], osem.at[h]
        )
        out.start()
        outs.append(out)
    for out in outs:
        out.wait()


def wgrad(lrow, lslot, lact, meta, own, other, pieces):
    vm = pl.BlockSpec(memory_space=pltpu.VMEM)
    anyspace = pl.BlockSpec(memory_space=pl.ANY)
    return pl.pallas_call(
        wgrad_kernel,
        out_shape=jax.ShapeDtypeStruct((SLOTS, 256, 128), BF),
        in_specs=[pl.BlockSpec(memory_space=pltpu.SMEM)] * 4 + [vm] * 2 + [anyspace] * 8,
        out_specs=anyspace,
        scratch_shapes=[
            pltpu.VMEM((128, TOK, 128), BF),
            pltpu.VMEM((1024, 2 * TOK), BF),
            pltpu.VMEM((SLOTS + 1, 256, 128), BF),
            pltpu.SemaphoreType.DMA((8,)),
            pltpu.SemaphoreType.DMA((2,)),
        ],
        compiler_params=pltpu.CompilerParams(vmem_limit_bytes=40 * 1024 * 1024),
        cost_estimate=pl.CostEstimate(flops=2 * 768 * 256 * 128 * 128, bytes_accessed=22 << 20, transcendentals=0),
        name="wgrad",
    )(lrow, lslot, lact, meta, own, other, *pieces)


def tables(block_rows, block_cols, block_count):
    i32 = jnp.int32
    c = lax.axis_index("c")
    x, z = lax.axis_index("x"), lax.axis_index("z")
    yh, yl = lax.axis_index("yh"), lax.axis_index("yl")
    sign = 1 - 2 * c
    slots = jnp.arange(SLOTS, dtype=i32)
    live = slots < block_count[0]
    row = block_rows % 4
    col = block_cols
    key = jnp.where(live, row * 64 + col, -1)
    hit = key[None, :] == jnp.arange(256, dtype=i32)[:, None]
    tab = jnp.min(jnp.where(hit, slots[None, :], SLOTS), axis=1)
    k = jnp.arange(4, dtype=i32)
    xs = (x - sign * k) % 4
    zs = (z - sign * k) % 4
    ys = yl ^ jnp.arange(2, dtype=i32)
    order = (((xs[:, None, None] * 4 + zs[None, :, None]) * 2 + ys[None, None, :]) * 2).reshape(32)
    half = slots // HALF
    same = (row[:, None] == row[None, :]) & (half[:, None] == half[None, :]) & live[None, :]
    rank = jnp.sum(jnp.where(same & (slots[None, :] < slots[:, None]), 1, 0), axis=1)
    count = jnp.sum(
        jnp.where(
            live[None, None, :]
            & (half[None, None, :] == jnp.arange(2, dtype=i32)[:, None, None])
            & (row[None, None, :] == k[None, :, None]),
            1,
            0,
        ),
        axis=2,
    )
    npair = (count + 1) // 2
    first = jnp.sum(jnp.where(k[None, :, None] > k[None, None, :], npair[:, None, :], 0), axis=2)
    mine = (jnp.arange(2, dtype=i32)[None, :, None] == half[:, None, None]) & (
        k[None, None, :] == row[:, None, None]
    )
    start = jnp.sum(jnp.where(mine, first[None], 0), axis=(1, 2))
    place = jnp.where(live, (half * PAIRS + start) * 2 + rank, -1)
    spots = jnp.arange(4 * PAIRS, dtype=i32)
    at = place[None, :] == spots[:, None]
    lslot = jnp.min(jnp.where(at, slots[None, :], SLOTS), axis=1)
    lrow = jnp.sum(jnp.where(at, row[None, :], 0), axis=1)
    lcol = jnp.sum(jnp.where(at, col[None, :], 0), axis=1)
    cx, cz, cy, par = lcol >> 4, (lcol >> 2) & 3, (lcol >> 1) & 1, lcol & 1
    kx = (sign * (x - cx)) % 4
    kz = (sign * (z - cz)) % 4
    lact = []
    for j in range(2):
        ky = (sign * ((yh * 2 + yl) - ((yh ^ j) * 2 + cy))) % 4
        lact.append(jnp.where(par == 0, ky * 16 + kz * 4 + kx, 64 + kz * 16 + ky * 4 + kx))
    lact = jnp.stack(lact, axis=1).reshape(-1)
    meta = jnp.concatenate([jnp.sum(npair, axis=1), block_count]).astype(i32)
    return tab, order, lrow, lslot, lact, meta


def after(value, *others):
    return lax.optimization_barrier((value, *others))[0]


def body(
    activations, gate_pre, up_pre, hidden_grad, gate_blocks, up_blocks, block_rows, block_cols, block_count,
):
    tab, order, lrow, lslot, lact, meta = tables(block_rows, block_cols, block_count)
    both = jnp.stack([activations[:, :128], activations[:, 128:]])
    near = [both] + [shift(both, "x", k) for k in (1, 2, 3)]
    gu, gut, t1 = first_terms(tab, order, gate_pre, up_pre, hidden_grad, gate_blocks, up_blocks)
    moving = shift(t1, "x", 1)
    other = shift(gut, "yh", 1)
    even = after(jnp.stack([v[0] for v in near]), t1)
    odd = after(jnp.stack([v[1] for v in near]), t1)
    evens, odds = [even], [odd]
    evens.append(shift(even, "z", 1))
    odds.append(shift(odd, "y", 1))
    t2, t3, t0 = rest_terms(tab, order, gu, gate_blocks, up_blocks)
    evens.append(shift(after(evens[1], t2), "z", 1))
    odds.append(shift(after(odds[1], t2), "y", 1))
    evens.append(shift(evens[2], "z", 1))
    odds.append(shift(odds[2], "y", 1))
    moving = add(moving, t2)
    evens = [after(jnp.concatenate(evens), moving, other)]
    odds = [after(jnp.concatenate(odds), moving, other)]
    moving = shift(moving, "x", 1)
    evens.append(shift(evens[0], "y", 1))
    odds.append(shift(odds[0], "z", 1))
    moving = add(moving, t3)
    evens.append(shift(after(evens[1], moving), "y", 1))
    odds.append(shift(after(odds[1], moving), "z", 1))
    moving = shift(moving, "x", 1)
    mine = add(moving, t0).reshape(4, 2, TOK, 256)
    evens.append(shift(after(evens[2], mine), "y", 1))
    odds.append(shift(after(odds[2], mine), "z", 1))
    moving = shift(mine[1], "z", 1)
    moving = add(moving, mine[2])
    meta = after(meta, moving)
    moving = shift(moving, "z", 1)
    moving = shift(add(moving, mine[3]), "z", 1)
    keep = moving[0].astype(F32) + mine[0, 0].astype(F32)
    send = add(moving[1], mine[0, 1])
    input_grad = (keep + shift(send, "yl", 1).astype(F32)).astype(BF)
    part = wgrad(lrow, lslot, lact, meta, gut, other, evens + odds)
    total = add(part, shift(part, "c", 1))
    return input_grad, total[:, :128], total[:, 128:]


def solution(mesh):
    fine = Mesh(mesh.devices.reshape(2, 2, 4, 4, 2), ("yh", "c", "x", "z", "yl"))
    tok, wt = ("yh", "c"), ("x", "z", "yl")
    in_specs = (P(tok, wt),) * 4 + (P(wt, None, None),) * 2 + (P(wt),) * 3
    out_specs = (P(tok, wt), P(wt, None, None), P(wt, None, None))
    return jax.shard_map(body, mesh=fine, in_specs=in_specs, out_specs=out_specs, check_vma=False)
```

```python
import functools

import jax
import jax.numpy as jnp
from jax import lax
from jax.experimental import pallas as pl
from jax.experimental.pallas import tpu as pltpu
from jax.sharding import Mesh
from jax.sharding import PartitionSpec as P

BF = jnp.bfloat16
F32 = jnp.float32
AXES = {"x": ("c", "x"), "z": ("c", "z"), "y": ("yh", "c", "yl")}
SIZES = {"yh": 2, "c": 2, "x": 4, "z": 4, "yl": 2}
TOK = 384
SLOTS = 128
HALF = 64
PAIRS = 36


def shift(value, axis, step):
    pairs = []
    if axis in ("yh", "c", "yl"):
        return lax.ppermute(value, axis, [(0, 1), (1, 0)])
    if axis == "y":
        for yh in range(2):
            for c in range(2):
                for yl in range(2):
                    y = (yh * 2 + yl + (step if c == 0 else -step)) % 4
                    pairs.append(((yh * 2 + c) * 2 + yl, ((y // 2) * 2 + c) * 2 + y % 2))
    else:
        for c in range(2):
            for a in range(4):
                b = (a + (step if c == 0 else -step)) % 4
                pairs.append((c * 4 + a, c * 4 + b))
    return lax.ppermute(value, AXES[axis], pairs)


def add(a, b):
    return (a.astype(F32) + b.astype(F32)).astype(BF)


def gates_kernel(gate_ref, up_ref, hid_ref, gu, gut):
    g = gate_ref[...].astype(F32)
    u = up_ref[...].astype(F32)
    h = hid_ref[...].astype(F32)
    sig = 1.0 / (1.0 + jnp.exp(-g))
    gg = h * u * sig * (1.0 + g * (1.0 - sig))
    ug = h * g * sig
    gu[:, :128] = gg.astype(BF)
    gu[:, 128:] = ug.astype(BF)
    gut[:128, :] = gg.T.astype(BF)
    gut[128:, :] = ug.T.astype(BF)


def chunk_kernel(k, tab, order, gu, wg, wu, out):
    @pl.loop(0, 8)
    def _(j):
        base = order[k * 8 + j]
        total = jnp.zeros((TOK, 256), F32)
        for r in range(4):
            sides = []
            for side in range(2):
                slot = tab[r * 64 + base + side]
                index = jnp.minimum(slot, SLOTS - 1)
                block = jnp.concatenate([wg[index], wu[index]], axis=0)
                sides.append(jnp.where(slot < SLOTS, block, jnp.zeros_like(block)))
            both = jnp.concatenate(sides, axis=1)
            total += jnp.dot(gu[:, r * 256 : (r + 1) * 256], both, preferred_element_type=F32)
        out[j] = total.astype(BF)


PIECE = jax.ShapeDtypeStruct((8, TOK, 256), BF)
VM = pl.BlockSpec(memory_space=pltpu.VMEM)
SM = pl.BlockSpec(memory_space=pltpu.SMEM)
ANY = pl.BlockSpec(memory_space=pl.ANY)


def gates(gate_pre, up_pre, hidden):
    return pl.pallas_call(
        gates_kernel,
        out_shape=[jax.ShapeDtypeStruct((TOK, 1024), BF), jax.ShapeDtypeStruct((1024, TOK), BF)],
        grid=(4,),
        in_specs=[pl.BlockSpec((TOK, 128), lambda r: (0, r))] * 3,
        out_specs=[pl.BlockSpec((TOK, 256), lambda r: (0, r)), pl.BlockSpec((256, TOK), lambda r: (r, 0))],
        compiler_params=pltpu.CompilerParams(vmem_limit_bytes=16 * 1024 * 1024),
        cost_estimate=pl.CostEstimate(flops=TOK * 512 * 20, bytes_accessed=3 << 20, transcendentals=TOK * 512),
        name="gates",
    )(gate_pre, up_pre, hidden)


def terms(k, tab, order, gu, wg, wu):
    return pl.pallas_call(
        functools.partial(chunk_kernel, k),
        out_shape=PIECE,
        in_specs=[SM] * 2 + [VM] * 3,
        out_specs=VM,
        compiler_params=pltpu.CompilerParams(vmem_limit_bytes=24 * 1024 * 1024),
        cost_estimate=pl.CostEstimate(flops=2 * TOK * 1024 * 2048, bytes_accessed=10 << 20, transcendentals=0),
        name="terms",
    )(tab, order, gu, wg, wu)


def wgrad_kernel(
    lrow, lslot, lact, meta, own_ref, other_ref, *rest,
):
    pieces, out_hbm = rest[:8], rest[8]
    acts, gt, stage, asem, osem = rest[9:]
    copies = [
        pltpu.make_async_copy(piece, acts.at[pl.ds(n * 16, 16)], asem.at[n]) for n, piece in enumerate(pieces)
    ]
    for copy in copies:
        copy.start()
    gt[:, :TOK] = own_ref[...]
    gt[:, TOK:] = other_ref[...]

    @pl.loop(meta[2], SLOTS)
    def _(s):
        stage[s] = jnp.zeros((256, 128), BF)

    for copy in copies:
        copy.wait()
    outs = []
    for h in range(2):

        @pl.loop(0, meta[h])
        def _(p):
            pos = (h * PAIRS + p) * 2
            rows = pl.ds(pl.multiple_of(lrow[pos] * 256, 256), 256)
            left = jnp.concatenate([acts[lact[pos * 2]], acts[lact[pos * 2 + 1]]], axis=0)
            right = jnp.concatenate([acts[lact[pos * 2 + 2]], acts[lact[pos * 2 + 3]]], axis=0)
            both = jnp.concatenate([left, right], axis=1)
            total = jnp.dot(gt[rows, :], both, preferred_element_type=F32).astype(BF)
            stage[lslot[pos]] = total[:, :128]
            stage[lslot[pos + 1]] = total[:, 128:]

        out = pltpu.make_async_copy(
            stage.at[pl.ds(h * HALF, HALF)], out_hbm.at[pl.ds(h * HALF, HALF)], osem.at[h]
        )
        out.start()
        outs.append(out)
    for out in outs:
        out.wait()


def wgrad(lrow, lslot, lact, meta, own, other, pieces):
    return pl.pallas_call(
        wgrad_kernel,
        out_shape=jax.ShapeDtypeStruct((SLOTS, 256, 128), BF),
        in_specs=[SM] * 4 + [VM] * 2 + [ANY] * 8,
        out_specs=ANY,
        scratch_shapes=[
            pltpu.VMEM((128, TOK, 128), BF),
            pltpu.VMEM((1024, 2 * TOK), BF),
            pltpu.VMEM((SLOTS + 1, 256, 128), BF),
            pltpu.SemaphoreType.DMA((8,)),
            pltpu.SemaphoreType.DMA((2,)),
        ],
        compiler_params=pltpu.CompilerParams(vmem_limit_bytes=40 * 1024 * 1024),
        cost_estimate=pl.CostEstimate(flops=2 * 768 * 256 * 128 * 128, bytes_accessed=22 << 20, transcendentals=0),
        name="wgrad",
    )(lrow, lslot, lact, meta, own, other, *pieces)


def tables(block_rows, block_cols, block_count):
    i32 = jnp.int32
    c = lax.axis_index("c")
    x, z = lax.axis_index("x"), lax.axis_index("z")
    yh, yl = lax.axis_index("yh"), lax.axis_index("yl")
    sign = 1 - 2 * c
    slots = jnp.arange(SLOTS, dtype=i32)
    live = slots < block_count[0]
    row = block_rows % 4
    col = block_cols
    key = jnp.where(live, row * 64 + col, -1)
    hit = key[None, :] == jnp.arange(256, dtype=i32)[:, None]
    tab = jnp.min(jnp.where(hit, slots[None, :], SLOTS), axis=1)
    k = jnp.arange(4, dtype=i32)
    xs = (x - sign * k) % 4
    zs = (z - sign * k) % 4
    ys = yl ^ jnp.arange(2, dtype=i32)
    order = (((xs[:, None, None] * 4 + zs[None, :, None]) * 2 + ys[None, None, :]) * 2).reshape(32)
    half = slots // HALF
    same = (row[:, None] == row[None, :]) & (half[:, None] == half[None, :]) & live[None, :]
    rank = jnp.sum(jnp.where(same & (slots[None, :] < slots[:, None]), 1, 0), axis=1)
    count = jnp.sum(
        jnp.where(
            live[None, None, :]
            & (half[None, None, :] == jnp.arange(2, dtype=i32)[:, None, None])
            & (row[None, None, :] == k[None, :, None]),
            1,
            0,
        ),
        axis=2,
    )
    npair = (count + 1) // 2
    first = jnp.sum(jnp.where(k[None, :, None] > k[None, None, :], npair[:, None, :], 0), axis=2)
    mine = (jnp.arange(2, dtype=i32)[None, :, None] == half[:, None, None]) & (
        k[None, None, :] == row[:, None, None]
    )
    start = jnp.sum(jnp.where(mine, first[None], 0), axis=(1, 2))
    place = jnp.where(live, (half * PAIRS + start) * 2 + rank, -1)
    spots = jnp.arange(4 * PAIRS, dtype=i32)
    at = place[None, :] == spots[:, None]
    lslot = jnp.min(jnp.where(at, slots[None, :], SLOTS), axis=1)
    lrow = jnp.sum(jnp.where(at, row[None, :], 0), axis=1)
    lcol = jnp.sum(jnp.where(at, col[None, :], 0), axis=1)
    cx, cz, cy, par = lcol >> 4, (lcol >> 2) & 3, (lcol >> 1) & 1, lcol & 1
    kx = (sign * (x - cx)) % 4
    kz = (sign * (z - cz)) % 4
    lact = []
    for j in range(2):
        ky = (sign * ((yh * 2 + yl) - ((yh ^ j) * 2 + cy))) % 4
        lact.append(jnp.where(par == 0, ky * 16 + kz * 4 + kx, 64 + kz * 16 + ky * 4 + kx))
    lact = jnp.stack(lact, axis=1).reshape(-1)
    meta = jnp.concatenate([jnp.sum(npair, axis=1), block_count]).astype(i32)
    return tab, order, lrow, lslot, lact, meta


def after(value, *others):
    return lax.optimization_barrier((value, *others))[0]


def body(
    activations, gate_pre, up_pre, hidden_grad, gate_blocks, up_blocks, block_rows, block_cols, block_count,
):
    tab, order, lrow, lslot, lact, meta = tables(block_rows, block_cols, block_count)
    both = jnp.stack([activations[:, :128], activations[:, 128:]])
    near = [both] + [shift(both, "x", k) for k in (1, 2, 3)]
    gu, gut = gates(gate_pre, up_pre, hidden_grad)
    other = shift(gut, "yh", 1)
    t1 = terms(1, tab, order, gu, gate_blocks, up_blocks)
    moving = shift(t1, "x", 1)
    even = after(jnp.stack([v[0] for v in near]), t1)
    odd = after(jnp.stack([v[1] for v in near]), t1)
    evens, odds = [even], [odd]
    evens.append(shift(even, "z", 1))
    odds.append(shift(odd, "y", 1))
    t2 = terms(2, tab, order, after(gu, even, odd), gate_blocks, up_blocks)
    evens.append(shift(after(evens[1], t2), "z", 1))
    odds.append(shift(after(odds[1], t2), "y", 1))
    t3 = terms(3, tab, order, after(gu, evens[1], odds[1]), gate_blocks, up_blocks)
    evens.append(shift(after(evens[2], t3, other), "z", 1))
    odds.append(shift(after(odds[2], t3, other), "y", 1))
    t0 = terms(0, tab, order, after(gu, evens[2], odds[2]), gate_blocks, up_blocks)
    moving = add(moving, t2)
    evens = [after(jnp.concatenate(evens), t0, moving)]
    odds = [after(jnp.concatenate(odds), t0, moving)]
    moving = shift(moving, "x", 1)
    evens.append(shift(evens[0], "y", 1))
    odds.append(shift(odds[0], "z", 1))
    moving = add(moving, t3)
    evens.append(shift(after(evens[1], moving), "y", 1))
    odds.append(shift(after(odds[1], moving), "z", 1))
    moving = shift(moving, "x", 1)
    mine = add(moving, t0).reshape(4, 2, TOK, 256)
    evens.append(shift(after(evens[2], mine), "y", 1))
    odds.append(shift(after(odds[2], mine), "z", 1))
    moving = shift(mine[1], "z", 1)
    moving = add(moving, mine[2])
    meta = after(meta, moving)
    moving = shift(moving, "z", 1)
    moving = shift(add(moving, mine[3]), "z", 1)
    keep = moving[0].astype(F32) + mine[0, 0].astype(F32)
    send = add(moving[1], mine[0, 1])
    input_grad = (keep + shift(send, "yl", 1).astype(F32)).astype(BF)
    part = wgrad(lrow, lslot, lact, meta, gut, other, evens + odds)
    total = add(part, shift(part, "c", 1))
    return input_grad, total[:, :128], total[:, 128:]


def solution(mesh):
    fine = Mesh(mesh.devices.reshape(2, 2, 4, 4, 2), ("yh", "c", "x", "z", "yl"))
    tok, wt = ("yh", "c"), ("x", "z", "yl")
    in_specs = (P(tok, wt),) * 4 + (P(wt, None, None),) * 2 + (P(wt),) * 3
    out_specs = (P(tok, wt), P(wt, None, None), P(wt, None, None))
    return jax.shard_map(body, mesh=fine, in_specs=in_specs, out_specs=out_specs, check_vma=False)
```

```python
import functools

import jax
import jax.numpy as jnp
from jax import lax
from jax.experimental import pallas as pl
from jax.experimental.pallas import tpu as pltpu
from jax.sharding import Mesh
from jax.sharding import PartitionSpec as P

BF = jnp.bfloat16
F32 = jnp.float32
AXES = {"x": ("c", "x"), "z": ("c", "z"), "y": ("yh", "c", "yl")}
SIZES = {"yh": 2, "c": 2, "x": 4, "z": 4, "yl": 2}
TOK = 384
SLOTS = 128
PAIRS = 76


def shift(value, axis, step):
    pairs = []
    if axis in ("yh", "c", "yl"):
        return lax.ppermute(value, axis, [(0, 1), (1, 0)])
    if axis == "y":
        for yh in range(2):
            for c in range(2):
                for yl in range(2):
                    y = (yh * 2 + yl + (step if c == 0 else -step)) % 4
                    pairs.append(((yh * 2 + c) * 2 + yl, ((y // 2) * 2 + c) * 2 + y % 2))
    else:
        for c in range(2):
            for a in range(4):
                b = (a + (step if c == 0 else -step)) % 4
                pairs.append((c * 4 + a, c * 4 + b))
    return lax.ppermute(value, AXES[axis], pairs)


def add(a, b):
    return (a.astype(F32) + b.astype(F32)).astype(BF)


def gates_kernel(gate_ref, up_ref, hid_ref, gu, gut):
    g = gate_ref[...].astype(F32)
    u = up_ref[...].astype(F32)
    h = hid_ref[...].astype(F32)
    sig = 1.0 / (1.0 + jnp.exp(-g))
    gg = h * u * sig * (1.0 + g * (1.0 - sig))
    ug = h * g * sig
    gu[:, :128] = gg.astype(BF)
    gu[:, 128:] = ug.astype(BF)
    gut[:128, :] = gg.T.astype(BF)
    gut[128:, :] = ug.T.astype(BF)


def chunk_kernel(k, tab, order, gu, wg, wu, out):
    @pl.loop(0, 8)
    def _(j):
        base = order[k * 8 + j]
        total = jnp.zeros((TOK, 256), F32)
        for r in range(4):
            sides = []
            for side in range(2):
                slot = tab[r * 64 + base + side]
                index = jnp.minimum(slot, SLOTS - 1)
                block = jnp.concatenate([wg[index], wu[index]], axis=0)
                sides.append(jnp.where(slot < SLOTS, block, jnp.zeros_like(block)))
            both = jnp.concatenate(sides, axis=1)
            total += jnp.dot(gu[:, r * 256 : (r + 1) * 256], both, preferred_element_type=F32)
        out[j] = total.astype(BF)


PIECE = jax.ShapeDtypeStruct((8, TOK, 256), BF)
VM = pl.BlockSpec(memory_space=pltpu.VMEM)
SM = pl.BlockSpec(memory_space=pltpu.SMEM)
ANY = pl.BlockSpec(memory_space=pl.ANY)


def gates(gate_pre, up_pre, hidden):
    return pl.pallas_call(
        gates_kernel,
        out_shape=[jax.ShapeDtypeStruct((TOK, 1024), BF), jax.ShapeDtypeStruct((1024, TOK), BF)],
        grid=(4,),
        in_specs=[pl.BlockSpec((TOK, 128), lambda r: (0, r))] * 3,
        out_specs=[pl.BlockSpec((TOK, 256), lambda r: (0, r)), pl.BlockSpec((256, TOK), lambda r: (r, 0))],
        compiler_params=pltpu.CompilerParams(vmem_limit_bytes=16 * 1024 * 1024),
        cost_estimate=pl.CostEstimate(flops=TOK * 512 * 20, bytes_accessed=3 << 20, transcendentals=TOK * 512),
        name="gates",
    )(gate_pre, up_pre, hidden)


def terms(k, tab, order, gu, wg, wu):
    return pl.pallas_call(
        functools.partial(chunk_kernel, k),
        out_shape=PIECE,
        in_specs=[SM] * 2 + [VM] * 3,
        out_specs=VM,
        compiler_params=pltpu.CompilerParams(vmem_limit_bytes=24 * 1024 * 1024),
        cost_estimate=pl.CostEstimate(flops=2 * TOK * 1024 * 2048, bytes_accessed=10 << 20, transcendentals=0),
        name="terms",
    )(tab, order, gu, wg, wu)


def put(block, grads, slot, sem):
    pltpu.make_async_copy(block, grads.at[slot], sem).start()


def finish(copies, zero, grads, sem):
    @pl.loop(0, copies)
    def _(_):
        pltpu.make_async_copy(zero, grads.at[0], sem).wait()


def same_row_pairs(low, high, refs, groups, lrow, lslot, ltile, gt, gate, up, gbuf, ubuf, sem):
    @pl.loop(low, high)
    def _(p):
        pos = p * 2
        rows = pl.ds(pl.multiple_of(lrow[pos] * 256, 256), 256)
        left = jnp.concatenate([gt[g, rows, :] for g in groups], axis=1)
        sides = []
        for side in range(2):
            tiles = [ref[ltile[(pos + side) * 4 + n]] for n, ref in enumerate(refs)]
            sides.append(jnp.concatenate(tiles, axis=0))
        total = jnp.dot(left, jnp.concatenate(sides, axis=1), preferred_element_type=F32).astype(BF)
        for side in range(2):
            gbuf[pos + side] = total[:128, side * 128 : side * 128 + 128]
            ubuf[pos + side] = total[128:, side * 128 : side * 128 + 128]
        put(gbuf.at[pos], gate, lslot[pos], sem)
        put(ubuf.at[pos], up, lslot[pos], sem)

        @pl.when(lslot[pos + 1] < SLOTS)
        def _():
            put(gbuf.at[pos + 1], gate, lslot[pos + 1], sem)
            put(ubuf.at[pos + 1], up, lslot[pos + 1], sem)


def early_kernel(
    lrow, lslot, ltile, meta, gt, e0, e2, o0, o2, e0c, e2c, o0c, o2c, gate, up, gbuf, ubuf, zero, sem
):
    zero[...] = jnp.zeros((128, 128), BF)

    @pl.loop(meta[8], SLOTS)
    def _(s):
        put(zero, gate, s, sem)
        put(zero, up, s, sem)

    lists = (lrow, lslot, ltile, gt, gate, up, gbuf, ubuf, sem)
    same_row_pairs(meta[0], meta[1], (e0, e2, e0c, e2c), (0, 1, 2, 3), *lists)
    same_row_pairs(meta[1], meta[2], (o0, o0, o0c, o0c), (0, 1, 2, 3), *lists)
    same_row_pairs(meta[2], meta[3], (o2, o2, o2c, o2c), (0, 1, 2, 3), *lists)
    finish(2 * (SLOTS - meta[9]), zero, gate, sem)


def late_kernel(
    lrow, lslot, ltile, meta, gt, e1, e3, o1, o3, e1c, e3c, o1c, o3c, gate_in, up_in, gate, up, gbuf, ubuf, zero, sem
):
    del gate_in, up_in
    lists = (lrow, lslot, ltile, gt, gate, up, gbuf, ubuf, sem)
    flip = meta[7]
    same_row_pairs(meta[3], meta[4], (e1, e3, e1c, e3c), (flip, 1 - flip, 3 - flip, 2 + flip), *lists)
    same_row_pairs(meta[4], meta[5], (o3, o3, o1c, o1c), (0, 1, 2, 3), *lists)
    same_row_pairs(meta[5], meta[6], (o1, o1, o3c, o3c), (0, 1, 2, 3), *lists)
    finish(2 * meta[9], zero, gate, sem)


def weight_grads(kernel, name, lists, gt, pieces, held=()):
    grads = jax.ShapeDtypeStruct((SLOTS, 128, 128), BF)
    return pl.pallas_call(
        kernel,
        out_shape=[grads] * 2,
        in_specs=[SM] * 4 + [VM] * 9 + [ANY] * len(held),
        out_specs=[ANY] * 2,
        scratch_shapes=[
            pltpu.VMEM((2 * PAIRS, 128, 128), BF),
            pltpu.VMEM((2 * PAIRS, 128, 128), BF),
            pltpu.VMEM((128, 128), BF),
            pltpu.SemaphoreType.DMA,
        ],
        input_output_aliases={13 + n: n for n in range(len(held))},
        compiler_params=pltpu.CompilerParams(vmem_limit_bytes=24 * 1024 * 1024),
        cost_estimate=pl.CostEstimate(flops=2 * 1536 * 256 * 128 * 64, bytes_accessed=22 << 20, transcendentals=0),
        name=name,
    )(*lists, gt, *pieces, *held)


def tables(block_rows, block_cols, block_count):
    i32 = jnp.int32
    x, z = lax.axis_index("x"), lax.axis_index("z")
    yh, yl = lax.axis_index("yh"), lax.axis_index("yl")
    sign = 1 - 2 * lax.axis_index("c")
    slots = jnp.arange(SLOTS, dtype=i32)
    live = slots < block_count[0]
    row = block_rows % 4
    col = block_cols
    key = jnp.where(live, row * 64 + col, -1)
    hit = key[None, :] == jnp.arange(256, dtype=i32)[:, None]
    tab = jnp.min(jnp.where(hit, slots[None, :], SLOTS), axis=1)
    k = jnp.arange(4, dtype=i32)
    xs = (x - sign * k) % 4
    zs = (z - sign * k) % 4
    ys = yl ^ jnp.arange(2, dtype=i32)
    order = (((xs[:, None, None] * 4 + zs[None, :, None]) * 2 + ys[None, None, :]) * 2).reshape(32)
    near = (sign * (z - (col >> 2))) % 4
    odd_kind = jnp.where(near == 0, 1, jnp.where(near == 2, 2, jnp.where(near == 3, 4, 5)))
    even_kind = jnp.where(((col >> 1) & 1) == yl, 0, 3)
    group = jnp.where((col & 1) == 0, even_kind, odd_kind) * 4 + row
    same = (group[:, None] == group[None, :]) & live[None, :]
    rank = jnp.sum(jnp.where(same & (slots[None, :] < slots[:, None]), 1, 0), axis=1)
    groups = jnp.arange(24, dtype=i32)
    count = jnp.sum(jnp.where((group[None, :] == groups[:, None]) & live[None, :], 1, 0), axis=1)
    npair = (count + 1) // 2
    edges = jnp.arange(7, dtype=i32) * 4
    bounds = jnp.sum(jnp.where(groups[None, :] < edges[:, None], npair[None, :], 0), axis=1)
    start = jnp.sum(jnp.where(groups[None, :] < group[:, None], npair[None, :], 0), axis=1)
    place = jnp.where(live, start * 2 + rank, -1)
    at = place[None, :] == jnp.arange(2 * PAIRS, dtype=i32)[:, None]
    lslot = jnp.min(jnp.where(at, slots[None, :], SLOTS), axis=1)
    lrow = jnp.sum(jnp.where(at, row[None, :], 0), axis=1)
    lcol = jnp.sum(jnp.where(at, col[None, :], 0), axis=1)
    cx, cz, cy, par = lcol >> 4, (lcol >> 2) & 3, (lcol >> 1) & 1, lcol & 1
    tiles = []
    for way in (sign, -sign):
        kx = (way * (x - cx)) % 4
        kz = (way * (z - cz)) % 4
        for j in range(2):
            ky = (way * ((yh * 2 + yl) - ((yh ^ j) * 2 + cy))) % 4
            tiles.append(jnp.where(par == 0, kz, ky) * 4 + kx)
    ltile = jnp.stack(tiles, axis=1).reshape(-1)
    flip = jnp.where((yl == 1) == (sign == 1), 0, 1).astype(i32)
    late = jnp.sum(jnp.where(live & (group >= 12), 1, 0))
    meta = jnp.concatenate([bounds, flip[None], block_count, late[None]]).astype(i32)
    return tab, order, lrow, lslot, ltile, meta


def after(value, *others):
    return lax.optimization_barrier((value, *others))[0]


def body(
    activations, gate_pre, up_pre, hidden_grad, gate_blocks, up_blocks, block_rows, block_cols, block_count,
):
    tab, order, lrow, lslot, ltile, meta = tables(block_rows, block_cols, block_count)
    both = jnp.stack([activations[:, :128], activations[:, 128:]])
    near = [both] + [shift(both, "x", k) for k in (1, 2, 3)]
    gu, gut = gates(gate_pre, up_pre, hidden_grad)
    other = shift(gut, "yh", 1)
    t1 = terms(1, tab, order, gu, gate_blocks, up_blocks)
    moving = shift(t1, "x", 1)
    even = after(jnp.stack([v[0] for v in near]), t1)
    odd = after(jnp.stack([v[1] for v in near]), t1, other)
    evens, odds = [even], [odd]
    evens.append(shift(even, "z", 1))
    odds.append(shift(odd, "y", 1))
    t2 = terms(2, tab, order, after(gu, even, odd), gate_blocks, up_blocks)
    evens.append(shift(after(evens[1], t2), "z", 1))
    odds.append(shift(after(odds[1], t2), "y", 1))
    t3 = terms(3, tab, order, after(gu, evens[1], odds[1]), gate_blocks, up_blocks)
    moving = add(moving, t2)
    evens.append(shift(after(evens[2], t3), "z", 1))
    odds.append(shift(after(odds[2], t3), "y", 1))
    moving = shift(moving, "x", 1)
    t0 = terms(0, tab, order, after(gu, evens[2], odds[2]), gate_blocks, up_blocks)
    own = jnp.stack([gut, other])
    gt = jnp.concatenate([own, shift(own, "c", 1)])
    evens = [after(jnp.concatenate(evens), t0)]
    odds = [after(jnp.concatenate(odds), t0)]
    evens.append(shift(evens[0], "y", 1))
    odds.append(shift(odds[0], "z", 1))
    evens_c = [shift(evens[0], "c", 1)]
    odds_c = [shift(odds[0], "c", 1)]
    moving = add(moving, t3)
    evens.append(shift(after(evens[1], moving, gt), "y", 1))
    odds.append(shift(after(odds[1], moving, evens_c[0], odds_c[0]), "z", 1))
    moving = shift(moving, "x", 1)
    evens_c.append(shift(evens[1], "c", 1))
    odds_c.append(shift(odds[1], "c", 1))
    mine = add(moving, t0).reshape(4, 2, TOK, 256)
    evens.append(shift(after(evens[2], mine, evens_c[1]), "y", 1))
    odds.append(shift(after(odds[2], mine, odds_c[1]), "z", 1))
    evens_c.append(shift(evens[2], "c", 1))
    odds_c.append(shift(odds[2], "c", 1))
    moving = shift(mine[1], "z", 1)
    moving = add(moving, mine[2])
    early = [v[n] for v in (evens, odds, evens_c, odds_c) for n in (0, 2)]
    grads = weight_grads(
        early_kernel, "early_grads", (lrow, lslot, ltile, after(meta, moving)), gt, early
    )
    moving = add(after(shift(moving, "z", 1), grads[0]), mine[3])
    moving = shift(moving, "z", 1)
    keep = moving[0].astype(F32) + mine[0, 0].astype(F32)
    send = add(moving[1], mine[0, 1])
    evens_c.append(shift(after(evens[3], send), "c", 1))
    odds_c.append(shift(after(odds[3], send), "c", 1))
    input_grad = (keep + shift(send, "yl", 1).astype(F32)).astype(BF)
    late = [v[n] for v in (evens, odds, evens_c, odds_c) for n in (1, 3)]
    gate_grad, up_grad = weight_grads(
        late_kernel, "late_grads", (lrow, lslot, ltile, after(meta, input_grad)), gt, late, grads
    )
    return input_grad, gate_grad, up_grad


def solution(mesh):
    fine = Mesh(mesh.devices.reshape(2, 2, 4, 4, 2), ("yh", "c", "x", "z", "yl"))
    tok, wt = ("yh", "c"), ("x", "z", "yl")
    in_specs = (P(tok, wt),) * 4 + (P(wt, None, None),) * 2 + (P(wt),) * 3
    out_specs = (P(tok, wt), P(wt, None, None), P(wt, None, None))
    return jax.shard_map(body, mesh=fine, in_specs=in_specs, out_specs=out_specs, check_vma=False)
```

```python
import functools

import jax
import jax.numpy as jnp
from jax import lax
from jax.experimental import pallas as pl
from jax.experimental.pallas import tpu as pltpu
from jax.sharding import Mesh
from jax.sharding import PartitionSpec as P

BF = jnp.bfloat16
F32 = jnp.float32
AXES = {"x": ("c", "x"), "z": ("c", "z"), "y": ("yh", "c", "yl")}
SIZES = {"yh": 2, "c": 2, "x": 4, "z": 4, "yl": 2}
TOK = 384
SLOTS = 128
PAIRS = 82


def shift(value, axis, step):
    pairs = []
    if axis in ("yh", "c", "yl"):
        return lax.ppermute(value, axis, [(0, 1), (1, 0)])
    if axis == "y":
        for yh in range(2):
            for c in range(2):
                for yl in range(2):
                    y = (yh * 2 + yl + (step if c == 0 else -step)) % 4
                    pairs.append(((yh * 2 + c) * 2 + yl, ((y // 2) * 2 + c) * 2 + y % 2))
    else:
        for c in range(2):
            for a in range(4):
                b = (a + (step if c == 0 else -step)) % 4
                pairs.append((c * 4 + a, c * 4 + b))
    return lax.ppermute(value, AXES[axis], pairs)


def add(a, b):
    return (a.astype(F32) + b.astype(F32)).astype(BF)


def gates_kernel(gate_ref, up_ref, hid_ref, gu, gut):
    g = gate_ref[...].astype(F32)
    u = up_ref[...].astype(F32)
    h = hid_ref[...].astype(F32)
    sig = 1.0 / (1.0 + jnp.exp(-g))
    gg = h * u * sig * (1.0 + g * (1.0 - sig))
    ug = h * g * sig
    gu[:, :128] = gg.astype(BF)
    gu[:, 128:] = ug.astype(BF)
    gut[:128, :] = gg.T.astype(BF)
    gut[128:, :] = ug.T.astype(BF)


def chunk_kernel(k, tab, order, gu, wg, wu, out):
    @pl.loop(0, 8)
    def _(j):
        base = order[k * 8 + j]
        total = jnp.zeros((TOK, 256), F32)
        for r in range(4):
            sides = []
            for side in range(2):
                slot = tab[r * 64 + base + side]
                index = jnp.minimum(slot, SLOTS - 1)
                block = jnp.concatenate([wg[index], wu[index]], axis=0)
                sides.append(jnp.where(slot < SLOTS, block, jnp.zeros_like(block)))
            both = jnp.concatenate(sides, axis=1)
            total += jnp.dot(gu[:, r * 256 : (r + 1) * 256], both, preferred_element_type=F32)
        out[j] = total.astype(BF)


PIECE = jax.ShapeDtypeStruct((8, TOK, 256), BF)
VM = pl.BlockSpec(memory_space=pltpu.VMEM)
SM = pl.BlockSpec(memory_space=pltpu.SMEM)
ANY = pl.BlockSpec(memory_space=pl.ANY)


def gates(gate_pre, up_pre, hidden):
    return pl.pallas_call(
        gates_kernel,
        out_shape=[jax.ShapeDtypeStruct((TOK, 1024), BF), jax.ShapeDtypeStruct((1024, TOK), BF)],
        grid=(4,),
        in_specs=[pl.BlockSpec((TOK, 128), lambda r: (0, r))] * 3,
        out_specs=[pl.BlockSpec((TOK, 256), lambda r: (0, r)), pl.BlockSpec((256, TOK), lambda r: (r, 0))],
        compiler_params=pltpu.CompilerParams(vmem_limit_bytes=16 * 1024 * 1024),
        cost_estimate=pl.CostEstimate(flops=1, bytes_accessed=1, transcendentals=0),
        name="gates",
    )(gate_pre, up_pre, hidden)


def terms(k, tab, order, gu, wg, wu):
    return pl.pallas_call(
        functools.partial(chunk_kernel, k),
        out_shape=PIECE,
        in_specs=[SM] * 2 + [VM] * 3,
        out_specs=VM,
        compiler_params=pltpu.CompilerParams(vmem_limit_bytes=8 * 1024 * 1024),
        cost_estimate=pl.CostEstimate(flops=1, bytes_accessed=1, transcendentals=0),
        name="terms",
    )(tab, order, gu, wg, wu)


def put(block, grads, slot, sem):
    pltpu.make_async_copy(block, grads.at[slot], sem).start()


def finish(copies, zero, grads, sem):
    @pl.loop(0, copies)
    def _(_):
        pltpu.make_async_copy(zero, grads.at[0], sem).wait()


def same_row_pairs(low, high, refs, groups, lrow, lslot, ltile, gt, gate, up, gbuf, ubuf, sem):
    @pl.loop(low, high)
    def _(step):
        for pair in range(2):
            pos = step * 4 + pair * 2
            rows = pl.ds(pl.multiple_of(lrow[pos] * 256, 256), 256)
            left = jnp.concatenate([gt[g, rows, :] for g in groups], axis=1)
            sides = []
            for side in range(2):
                tiles = [ref[ltile[(pos + side) * 4 + n]] for n, ref in enumerate(refs)]
                sides.append(jnp.concatenate(tiles, axis=0))
            total = jnp.dot(left, jnp.concatenate(sides, axis=1), preferred_element_type=F32).astype(BF)
            for side in range(2):
                gbuf[pos + side] = total[:128, side * 128 : side * 128 + 128]
                ubuf[pos + side] = total[128:, side * 128 : side * 128 + 128]
        for n in range(4):
            pos = step * 4 + n

            @pl.when(lslot[pos] < SLOTS)
            def _():
                put(gbuf.at[pos], gate, lslot[pos], sem)
                put(ubuf.at[pos], up, lslot[pos], sem)


def early_kernel(
    lrow, lslot, ltile, meta, gt, p0, p2, p0c, p2c, gate, up, gbuf, ubuf, zero, sem
):
    zero[...] = jnp.zeros((128, 128), BF)

    @pl.loop(meta[8], SLOTS)
    def _(s):
        put(zero, gate, s, sem)
        put(zero, up, s, sem)

    lists = (lrow, lslot, ltile, gt, gate, up, gbuf, ubuf, sem)
    same_row_pairs(meta[0], meta[1], (p0, p2, p0c, p2c), (0, 1, 2, 3), *lists)
    same_row_pairs(meta[1], meta[2], (p0, p0, p0c, p0c), (0, 1, 2, 3), *lists)
    same_row_pairs(meta[2], meta[3], (p2, p2, p2c, p2c), (0, 1, 2, 3), *lists)
    finish(2 * (SLOTS - meta[9]), zero, gate, sem)


def late_kernel(
    lrow, lslot, ltile, meta, gt, p1, p3, p1c, p3c, gate_in, up_in, gate, up, gbuf, ubuf, zero, sem
):
    del gate_in, up_in
    lists = (lrow, lslot, ltile, gt, gate, up, gbuf, ubuf, sem)
    flip = meta[7]
    same_row_pairs(meta[3], meta[4], (p1, p3, p1c, p3c), (flip, 1 - flip, 3 - flip, 2 + flip), *lists)
    same_row_pairs(meta[4], meta[5], (p3, p3, p1c, p1c), (0, 1, 2, 3), *lists)
    same_row_pairs(meta[5], meta[6], (p1, p1, p3c, p3c), (0, 1, 2, 3), *lists)
    finish(2 * meta[9], zero, gate, sem)


def weight_grads(kernel, name, lists, gt, pieces, held=()):
    grads = jax.ShapeDtypeStruct((SLOTS, 128, 128), BF)
    return pl.pallas_call(
        kernel,
        out_shape=[grads] * 2,
        in_specs=[SM] * 4 + [VM] * 5 + [ANY] * len(held),
        out_specs=[ANY] * 2,
        scratch_shapes=[
            pltpu.VMEM((2 * PAIRS, 128, 128), BF),
            pltpu.VMEM((2 * PAIRS, 128, 128), BF),
            pltpu.VMEM((128, 128), BF),
            pltpu.SemaphoreType.DMA,
        ],
        input_output_aliases={9 + n: n for n in range(len(held))},
        compiler_params=pltpu.CompilerParams(vmem_limit_bytes=28 * 1024 * 1024),
        cost_estimate=pl.CostEstimate(flops=1, bytes_accessed=1, transcendentals=0),
        name=name,
    )(*lists, gt, *pieces, *held)


def tables(block_rows, block_cols, block_count):
    i32 = jnp.int32
    x, z = lax.axis_index("x"), lax.axis_index("z")
    yh, yl = lax.axis_index("yh"), lax.axis_index("yl")
    sign = 1 - 2 * lax.axis_index("c")
    slots = jnp.arange(SLOTS, dtype=i32)
    live = slots < block_count[0]
    row = block_rows % 4
    col = block_cols
    key = jnp.where(live, row * 64 + col, -1)
    hit = key[None, :] == jnp.arange(256, dtype=i32)[:, None]
    tab = jnp.min(jnp.where(hit, slots[None, :], SLOTS), axis=1)
    k = jnp.arange(4, dtype=i32)
    xs = (x - sign * k) % 4
    zs = (z - sign * k) % 4
    ys = yl ^ jnp.arange(2, dtype=i32)
    order = (((xs[:, None, None] * 4 + zs[None, :, None]) * 2 + ys[None, None, :]) * 2).reshape(32)
    near = (sign * (z - (col >> 2))) % 4
    odd_kind = jnp.where(near == 0, 1, jnp.where(near == 2, 2, jnp.where(near == 3, 4, 5)))
    even_kind = jnp.where(((col >> 1) & 1) == yl, 0, 3)
    group = jnp.where((col & 1) == 0, even_kind, odd_kind) * 4 + row
    same = (group[:, None] == group[None, :]) & live[None, :]
    rank = jnp.sum(jnp.where(same & (slots[None, :] < slots[:, None]), 1, 0), axis=1)
    groups = jnp.arange(24, dtype=i32)
    count = jnp.sum(jnp.where((group[None, :] == groups[:, None]) & live[None, :], 1, 0), axis=1)
    npair = (count + 1) // 2
    kinds = jnp.arange(6, dtype=i32)
    steps = (jnp.sum(npair.reshape(6, 4), axis=1) + 1) // 2
    edges = jnp.arange(7, dtype=i32)
    bounds = jnp.sum(jnp.where(kinds[None, :] < edges[:, None], steps[None, :], 0), axis=1)
    kind = group // 4
    start = jnp.sum(jnp.where(kinds[None, :] < kind[:, None], 2 * steps[None, :], 0), axis=1) + jnp.sum(
        jnp.where((groups[None, :] < group[:, None]) & (groups[None, :] // 4 == kind[:, None]), npair[None, :], 0),
        axis=1,
    )
    place = jnp.where(live, start * 2 + rank, -1)
    at = place[None, :] == jnp.arange(2 * PAIRS, dtype=i32)[:, None]
    lslot = jnp.min(jnp.where(at, slots[None, :], SLOTS), axis=1)
    lrow = jnp.sum(jnp.where(at, row[None, :], 0), axis=1)
    lcol = jnp.sum(jnp.where(at, col[None, :], 0), axis=1)
    cx, cz, cy, par = lcol >> 4, (lcol >> 2) & 3, (lcol >> 1) & 1, lcol & 1
    tiles = []
    for way in (sign, -sign):
        kx = (way * (x - cx)) % 4
        kz = (way * (z - cz)) % 4
        for j in range(2):
            ky = (way * ((yh * 2 + yl) - ((yh ^ j) * 2 + cy))) % 4
            tiles.append(jnp.where(par == 0, kz, 4 + ky) * 4 + kx)
    ltile = jnp.stack(tiles, axis=1).reshape(-1)
    flip = jnp.where((yl == 1) == (sign == 1), 0, 1).astype(i32)
    late = jnp.sum(jnp.where(live & (group >= 12), 1, 0))
    meta = jnp.concatenate([bounds, flip[None], block_count, late[None]]).astype(i32)
    return tab, order, lrow, lslot, ltile, meta


def after(value, *others):
    return lax.optimization_barrier((value, *others))[0]


def body(
    activations, gate_pre, up_pre, hidden_grad, gate_blocks, up_blocks, block_rows, block_cols, block_count,
):
    tab, order, lrow, lslot, ltile, meta = tables(block_rows, block_cols, block_count)
    both = jnp.stack([activations[:, :128], activations[:, 128:]])
    near = [both] + [shift(both, "x", k) for k in (1, 2, 3)]
    gu, gut = gates(gate_pre, up_pre, hidden_grad)
    other = shift(gut, "yh", 1)
    even = jnp.stack([v[0] for v in near])
    odd = after(jnp.stack([v[1] for v in near]), other)
    even_1 = shift(even, "z", 1)
    odd_1 = shift(odd, "y", 1)
    t1 = terms(1, tab, order, after(gu, even_1), gate_blocks, up_blocks)
    moving = shift(t1, "x", 1)
    even_2 = shift(even_1, "z", 1)
    odd_2 = shift(after(odd_1, t1), "y", 1)
    even_a = [after(jnp.concatenate([even, even_1]), other)]
    odd_a = [after(jnp.concatenate([odd, odd_1]), t1)]
    even_a.append(shift(even_a[0], "y", 1))
    odd_a.append(shift(odd_a[0], "z", 1))
    even_3 = shift(even_2, "z", 1)
    odd_3 = shift(odd_2, "y", 1)
    t2 = terms(2, tab, order, after(gu, even_2, odd_1), gate_blocks, up_blocks)
    even_a.append(shift(after(even_a[1], t2), "y", 1))
    odd_a.append(shift(after(odd_a[1], t2), "z", 1))
    moving = add(moving, t2)
    even_b = [after(jnp.concatenate([even_2, even_3]), even_a[1], moving)]
    odd_b = [after(jnp.concatenate([odd_2, odd_3]), odd_a[1], moving)]
    moving = shift(moving, "x", 1)
    even_b.append(shift(even_b[0], "y", 1))
    odd_b.append(shift(odd_b[0], "z", 1))
    t3 = terms(3, tab, order, after(gu, even_a[1], odd_a[1]), gate_blocks, up_blocks)
    own = jnp.stack([gut, other])
    gt = jnp.concatenate([own, shift(own, "c", 1)])
    piece = [jnp.concatenate([even_a[0], even_b[0], odd_a[0], odd_b[0]])]
    piece_c = [shift(piece[0], "c", 1)]
    even_a.append(shift(after(even_a[2], t3), "y", 1))
    odd_a.append(shift(after(odd_a[2], t3), "z", 1))
    t0 = terms(0, tab, order, after(gu, even_a[2], odd_a[2]), gate_blocks, up_blocks)
    moving = add(moving, t3)
    even_b.append(shift(after(even_b[1], even_a[2], gt, moving, t0), "y", 1))
    odd_b.append(shift(after(odd_b[1], odd_a[2], gt, moving, t0), "z", 1))
    moving = shift(moving, "x", 1)
    for k in (1, 2):
        piece.append(jnp.concatenate([even_a[k], even_b[k], odd_a[k], odd_b[k]]))
        piece_c.append(shift(piece[k], "c", 1))
    even_b.append(shift(after(even_b[2], even_a[3], piece_c[0], piece_c[1]), "y", 1))
    odd_b.append(shift(after(odd_b[2], odd_a[3], piece_c[0], piece_c[1]), "z", 1))
    part_a = shift(jnp.concatenate([even_a[3], odd_a[3]]), "c", 1)
    mine = add(moving, t0).reshape(4, 2, TOK, 256)
    moving = shift(mine[1], "z", 1)
    grads = weight_grads(
        early_kernel,
        "early_grads",
        (lrow, lslot, ltile, after(meta, mine)),
        gt,
        (piece[0], piece[2], piece_c[0], piece_c[2]),
    )
    moving = add(after(moving, grads[0]), mine[2])
    moving = shift(moving, "z", 1)
    part_b = shift(jnp.concatenate([even_b[3], odd_b[3]]), "c", 1)
    moving = add(moving, mine[3])
    moving = shift(moving, "z", 1)
    piece.append(jnp.concatenate([even_a[3], even_b[3], odd_a[3], odd_b[3]]))
    piece_c.append(jnp.concatenate([part_a[:8], part_b[:8], part_a[8:], part_b[8:]]))
    gate_grad, up_grad = weight_grads(
        late_kernel, "late_grads", (lrow, lslot, ltile, meta), gt, (piece[1], piece[3], piece_c[1], piece_c[3]), grads
    )
    keep = moving[0].astype(F32) + mine[0, 0].astype(F32)
    send = add(moving[1], mine[0, 1])
    input_grad = (keep + shift(send, "yl", 1).astype(F32)).astype(BF)
    return input_grad, gate_grad, up_grad


def solution(mesh):
    fine = Mesh(mesh.devices.reshape(2, 2, 4, 4, 2), ("yh", "c", "x", "z", "yl"))
    tok, wt = ("yh", "c"), ("x", "z", "yl")
    in_specs = (P(tok, wt),) * 4 + (P(wt, None, None),) * 2 + (P(wt),) * 3
    out_specs = (P(tok, wt), P(wt, None, None), P(wt, None, None))
    return jax.shard_map(body, mesh=fine, in_specs=in_specs, out_specs=out_specs, check_vma=False)
```

```python
import functools

import jax
import jax.numpy as jnp
from jax import lax
from jax.experimental import pallas as pl
from jax.experimental.pallas import tpu as pltpu
from jax.sharding import Mesh
from jax.sharding import PartitionSpec as P

BF = jnp.bfloat16
F32 = jnp.float32
AXES = {"x": ("c", "x"), "z": ("c", "z"), "y": ("yh", "c", "yl")}
SIZES = {"yh": 2, "c": 2, "x": 4, "z": 4, "yl": 2}
TOK = 384
SLOTS = 128
PAIRS = 82


def shift(value, axis, step):
    pairs = []
    if axis in ("yh", "c", "yl"):
        return lax.ppermute(value, axis, [(0, 1), (1, 0)])
    if axis == "y":
        for yh in range(2):
            for c in range(2):
                for yl in range(2):
                    y = (yh * 2 + yl + (step if c == 0 else -step)) % 4
                    pairs.append(((yh * 2 + c) * 2 + yl, ((y // 2) * 2 + c) * 2 + y % 2))
    else:
        for c in range(2):
            for a in range(4):
                b = (a + (step if c == 0 else -step)) % 4
                pairs.append((c * 4 + a, c * 4 + b))
    return lax.ppermute(value, AXES[axis], pairs)


def add(a, b):
    return (a.astype(F32) + b.astype(F32)).astype(BF)


def sum_of(a, b, c):
    return (a.astype(F32) + b.astype(F32) + c.astype(F32)).astype(BF)


def gates_kernel(gate_ref, up_ref, hid_ref, gu, gut):
    g = gate_ref[...].astype(F32)
    u = up_ref[...].astype(F32)
    h = hid_ref[...].astype(F32)
    sig = 1.0 / (1.0 + jnp.exp(-g))
    gg = h * u * sig * (1.0 + g * (1.0 - sig))
    ug = h * g * sig
    gu[:, :128] = gg.astype(BF)
    gu[:, 128:] = ug.astype(BF)
    gut[:128, :] = gg.T.astype(BF)
    gut[128:, :] = ug.T.astype(BF)


def chunk_kernel(k, tab, order, gu, wg, wu, out):
    @pl.loop(0, 8)
    def _(j):
        base = order[k * 8 + j]
        total = jnp.zeros((TOK, 256), F32)
        for r in range(4):
            sides = []
            for side in range(2):
                slot = tab[r * 64 + base + side]
                index = jnp.minimum(slot, SLOTS - 1)
                block = jnp.concatenate([wg[index], wu[index]], axis=0)
                sides.append(jnp.where(slot < SLOTS, block, jnp.zeros_like(block)))
            both = jnp.concatenate(sides, axis=1)
            total += jnp.dot(gu[:, r * 256 : (r + 1) * 256], both, preferred_element_type=F32)
        out[j] = total.astype(BF)


PIECE = jax.ShapeDtypeStruct((8, TOK, 256), BF)
VM = pl.BlockSpec(memory_space=pltpu.VMEM)
SM = pl.BlockSpec(memory_space=pltpu.SMEM)
ANY = pl.BlockSpec(memory_space=pl.ANY)


def gates(gate_pre, up_pre, hidden):
    return pl.pallas_call(
        gates_kernel,
        out_shape=[jax.ShapeDtypeStruct((TOK, 1024), BF), jax.ShapeDtypeStruct((1024, TOK), BF)],
        grid=(4,),
        in_specs=[pl.BlockSpec((TOK, 128), lambda r: (0, r))] * 3,
        out_specs=[pl.BlockSpec((TOK, 256), lambda r: (0, r)), pl.BlockSpec((256, TOK), lambda r: (r, 0))],
        compiler_params=pltpu.CompilerParams(vmem_limit_bytes=16 * 1024 * 1024),
        cost_estimate=pl.CostEstimate(flops=1, bytes_accessed=1, transcendentals=0),
        name="gates",
    )(gate_pre, up_pre, hidden)


def terms(k, tab, order, gu, wg, wu):
    return pl.pallas_call(
        functools.partial(chunk_kernel, k),
        out_shape=PIECE,
        in_specs=[SM] * 2 + [VM] * 3,
        out_specs=VM,
        compiler_params=pltpu.CompilerParams(vmem_limit_bytes=8 * 1024 * 1024),
        cost_estimate=pl.CostEstimate(flops=1, bytes_accessed=1, transcendentals=0),
        name="terms",
    )(tab, order, gu, wg, wu)


def put(block, grads, slot, sem):
    pltpu.make_async_copy(block, grads.at[slot], sem).start()


def finish(copies, zero, grads, sem):
    @pl.loop(0, copies)
    def _(_):
        pltpu.make_async_copy(zero, grads.at[0], sem).wait()


def same_row_pairs(kind, origin, refs, groups, lrow, lslot, ltile, meta, gt, gate, up, gbuf, ubuf, sem):
    @pl.loop(meta[kind], meta[kind + 1])
    def _(step):
        for pair in range(2):
            pos = step * 4 + pair * 2
            rows = pl.ds(pl.multiple_of(lrow[pos] * 256, 256), 256)
            left = jnp.concatenate([gt[g, rows, :] for g in groups], axis=1)
            sides = []
            for side in range(2):
                tiles = [ref[ltile[(pos + side) * 4 + n]] for n, ref in enumerate(refs)]
                sides.append(jnp.concatenate(tiles, axis=0))
            total = jnp.dot(left, jnp.concatenate(sides, axis=1), preferred_element_type=F32).astype(BF)
            for side in range(2):
                gbuf[pos + side - origin] = total[:128, side * 128 : side * 128 + 128]
                ubuf[pos + side - origin] = total[128:, side * 128 : side * 128 + 128]
        for n in range(4):
            pos = step * 4 + n

            @pl.when(lslot[pos] < SLOTS)
            def _():
                put(gbuf.at[pos - origin], gate, lslot[pos], sem)
                put(ubuf.at[pos - origin], up, lslot[pos], sem)


def kinds_kernel(kinds, held, lrow, lslot, ltile, meta, gt, *rest):
    pieces, (gate, up, gbuf, ubuf, zero, sem) = rest[: len(rest) - 6 - held], rest[-6:]
    origin = meta[kinds[0][0]] * 4
    if not held:
        zero[...] = jnp.zeros((128, 128), BF)

        @pl.loop(meta[8], SLOTS)
        def _(s):
            put(zero, gate, s, sem)
            put(zero, up, s, sem)

        finish(2 * (SLOTS - meta[8]), zero, gate, sem)
    for kind, picks in kinds:
        refs = [pieces[n] for n in picks]
        flip = meta[7]
        groups = (flip, 1 - flip, 3 - flip, 2 + flip) if kind == 3 else (0, 1, 2, 3)
        same_row_pairs(kind, origin, refs, groups, lrow, lslot, ltile, meta, gt, gate, up, gbuf, ubuf, sem)
    finish(2 * (meta[9 + kinds[-1][0] + 1] - meta[9 + kinds[0][0]]), zero, gate, sem)


def weight_grads(name, kinds, room, lists, gt, pieces, held=()):
    grads = jax.ShapeDtypeStruct((SLOTS, 128, 128), BF)
    first = 5 + len(pieces)
    return pl.pallas_call(
        functools.partial(kinds_kernel, kinds, len(held)),
        out_shape=[grads] * 2,
        in_specs=[SM] * 4 + [VM] * (1 + len(pieces)) + [ANY] * len(held),
        out_specs=[ANY] * 2,
        scratch_shapes=[
            pltpu.VMEM((room, 128, 128), BF),
            pltpu.VMEM((room, 128, 128), BF),
            pltpu.VMEM((128, 128), BF),
            pltpu.SemaphoreType.DMA,
        ],
        input_output_aliases={first + n: n for n in range(len(held))},
        compiler_params=pltpu.CompilerParams(vmem_limit_bytes=25 * 1024 * 1024),
        cost_estimate=pl.CostEstimate(flops=1, bytes_accessed=1, transcendentals=0),
        name=name,
    )(*lists, gt, *pieces, *held)


def block_table(block_rows, block_cols, block_count):
    i32 = jnp.int32
    x, z, yl = lax.axis_index("x"), lax.axis_index("z"), lax.axis_index("yl")
    sign = 1 - 2 * lax.axis_index("c")
    slots = jnp.arange(SLOTS, dtype=i32)
    key = jnp.where(slots < block_count[0], block_rows % 4 * 64 + block_cols, -1)
    hit = key[None, :] == jnp.arange(256, dtype=i32)[:, None]
    tab = jnp.min(jnp.where(hit, slots[None, :], SLOTS), axis=1)
    k = jnp.arange(4, dtype=i32)
    xs = (x - sign * k) % 4
    zs = (z - sign * k) % 4
    ys = yl ^ jnp.arange(2, dtype=i32)
    order = (((xs[:, None, None] * 4 + zs[None, :, None]) * 2 + ys[None, None, :]) * 2).reshape(32)
    return tab, order


def slot_lists(block_rows, block_cols, block_count):
    i32 = jnp.int32
    x, z = lax.axis_index("x"), lax.axis_index("z")
    yh, yl = lax.axis_index("yh"), lax.axis_index("yl")
    sign = 1 - 2 * lax.axis_index("c")
    slots = jnp.arange(SLOTS, dtype=i32)
    live = slots < block_count[0]
    row = block_rows % 4
    col = block_cols
    near = (sign * (z - (col >> 2))) % 4
    odd_kind = jnp.where(near == 0, 0, jnp.where(near == 3, 1, jnp.where(near == 1, 2, 5)))
    even_kind = jnp.where(((col >> 1) & 1) == yl, 4, 3)
    kind = jnp.where((col & 1) == 0, even_kind, odd_kind)
    group = kind * 4 + row
    same = (group[:, None] == group[None, :]) & live[None, :]
    rank = jnp.sum(jnp.where(same & (slots[None, :] < slots[:, None]), 1, 0), axis=1)
    groups = jnp.arange(24, dtype=i32)
    count = jnp.sum(jnp.where((group[None, :] == groups[:, None]) & live[None, :], 1, 0), axis=1)
    npair = (count + 1) // 2
    kinds = jnp.arange(6, dtype=i32)
    steps = (jnp.sum(npair.reshape(6, 4), axis=1) + 1) // 2
    edges = jnp.arange(7, dtype=i32)
    before = kinds[None, :] < edges[:, None]
    bounds = jnp.sum(jnp.where(before, steps[None, :], 0), axis=1)
    lives = jnp.sum(jnp.where(before, jnp.sum(count.reshape(6, 4), axis=1)[None, :], 0), axis=1)
    start = jnp.sum(jnp.where(kinds[None, :] < kind[:, None], 2 * steps[None, :], 0), axis=1) + jnp.sum(
        jnp.where((groups[None, :] < group[:, None]) & (groups[None, :] // 4 == kind[:, None]), npair[None, :], 0),
        axis=1,
    )
    place = jnp.where(live, start * 2 + rank, -1)
    at = place[None, :] == jnp.arange(2 * PAIRS, dtype=i32)[:, None]
    lslot = jnp.min(jnp.where(at, slots[None, :], SLOTS), axis=1)
    lrow = jnp.sum(jnp.where(at, row[None, :], 0), axis=1)
    lcol = jnp.sum(jnp.where(at, col[None, :], 0), axis=1)
    cx, cz, cy, par = lcol >> 4, (lcol >> 2) & 3, (lcol >> 1) & 1, lcol & 1
    tiles = []
    for way in (sign, -sign):
        kx = (way * (x - cx)) % 4
        kz = (way * (z - cz)) % 4
        for j in range(2):
            ky = (way * ((yh * 2 + yl) - ((yh ^ j) * 2 + cy))) % 4
            tiles.append(jnp.where(par == 0, kz, ky) * 4 + kx)
    ltile = jnp.stack(tiles, axis=1).reshape(-1)
    flip = jnp.where((yl == 1) == (sign == 1), 0, 1).astype(i32)
    meta = jnp.concatenate([bounds, flip[None], block_count, lives]).astype(i32)
    return lrow, lslot, ltile, meta


def after(value, *others):
    return lax.optimization_barrier((value, *others))[0]


def body(
    activations, gate_pre, up_pre, hidden_grad, gate_blocks, up_blocks, block_rows, block_cols, block_count,
):
    tab, order = block_table(block_rows, block_cols, block_count)
    blocks = (gate_blocks, up_blocks)
    gu, gut = gates(gate_pre, up_pre, hidden_grad)
    other = shift(gut, "yh", 1)
    both = after(jnp.stack([activations[:, :128], activations[:, 128:]]), gut)
    near = [both] + [shift(both, "x", k) for k in (1, 2, 3)]
    t2 = terms(2, tab, order, gu, *blocks)
    ahead = shift(t2, "x", 1)
    even = after(jnp.stack([v[0] for v in near]), t2)
    odd = after(jnp.stack([v[1] for v in near]), t2, other)
    evens, odds = [even], [odd]
    evens.append(shift(even, "z", 1))
    odds.append(shift(odd, "y", 1))
    t1 = terms(1, tab, order, after(gu, even, odd), *blocks)
    back = shift(t1, "x", -1)
    evens.append(shift(after(evens[1], t1), "z", 1))
    odds.append(shift(after(odds[1], t1), "y", 1))
    t3 = terms(3, tab, order, after(gu, evens[1], odds[1]), *blocks)
    evens.append(shift(after(evens[2], t3), "z", 1))
    odds.append(shift(after(odds[2], t3), "y", 1))
    t0 = terms(0, tab, order, after(gu, evens[2], odds[2]), *blocks)
    moving = add(ahead, t3)
    even_0 = after(jnp.concatenate(evens), t0, moving)
    odd_0 = after(jnp.concatenate(odds), t0, moving)
    even_1, even_3 = shift(even_0, "y", 1), shift(even_0, "y", -1)
    odd_1, odd_3 = shift(odd_0, "z", 1), shift(odd_0, "z", -1)
    ahead = shift(moving, "x", 1)
    rows_late, cols_late, count_late = (after(v, even_0, odd_0) for v in (block_rows, block_cols, block_count))
    lrow, lslot, ltile, meta = slot_lists(rows_late, cols_late, count_late)
    mine = sum_of(t0, ahead, back).reshape(4, 2, TOK, 256)
    own = after(jnp.stack([gut, other]), mine)
    gt = jnp.concatenate([own, shift(own, "c", 1)])
    odd_0c = shift(after(odd_0, mine), "c", 1)

    def grads_of(name, kinds, room, pieces, held=(), wait=()):
        return weight_grads(name, kinds, room, (lrow, lslot, ltile, after(meta, *wait)), gt, pieces, held)

    even_2 = shift(after(even_1, even_3), "y", 1)
    odd_2 = shift(after(odd_1, odd_3), "z", 1)
    odd_1c, odd_3c = shift(odd_1, "c", 1), shift(odd_3, "c", 1)
    even_1c, even_3c = shift(after(even_1, odd_1c), "c", 1), shift(after(even_3, odd_1c), "c", 1)
    grads = grads_of(
        "grads_0_1_2",
        ((0, (0, 0, 1, 1)), (1, (3, 3, 4, 4)), (2, (2, 2, 5, 5))),
        116,
        (odd_0, odd_0c, odd_1, odd_3, odd_1c, odd_3c),
    )
    even_0c = shift(after(even_0, grads[0]), "c", 1)
    ahead = shift(after(mine[2], grads[0]), "z", 1)
    back = shift(after(mine[1], grads[0]), "z", -1)
    ahead = add(ahead, mine[3])
    grads = grads_of(
        "grads_3", ((3, (0, 1, 2, 3)),), 72, (even_1, even_3, even_1c, even_3c), grads, (even_2, odd_2, ahead)
    )
    even_2c, odd_2c = shift(even_2, "c", 1), shift(odd_2, "c", 1)
    ahead = shift(ahead, "z", 1)
    send = sum_of(mine[0, 1], ahead[1], back[1])
    keep = mine[0, 0].astype(F32) + ahead[0].astype(F32) + back[0].astype(F32)
    gate_grad, up_grad = grads_of(
        "grads_4_5",
        ((4, (0, 1, 2, 3)), (5, (4, 4, 5, 5))),
        108,
        (even_0, even_2, even_0c, even_2c, odd_2, odd_2c),
        grads,
        (send,),
    )
    input_grad = (keep + after(shift(send, "yl", 1), gate_grad).astype(F32)).astype(BF)
    return input_grad, gate_grad, up_grad


def solution(mesh):
    fine = Mesh(mesh.devices.reshape(2, 2, 4, 4, 2), ("yh", "c", "x", "z", "yl"))
    tok, wt = ("yh", "c"), ("x", "z", "yl")
    in_specs = (P(tok, wt),) * 4 + (P(wt, None, None),) * 2 + (P(wt),) * 3
    out_specs = (P(tok, wt), P(wt, None, None), P(wt, None, None))
    return jax.shard_map(body, mesh=fine, in_specs=in_specs, out_specs=out_specs, check_vma=False)
```

```python
import functools

import jax
import jax.numpy as jnp
from jax import lax
from jax.experimental import pallas as pl
from jax.experimental.pallas import tpu as pltpu
from jax.sharding import Mesh
from jax.sharding import PartitionSpec as P

BF = jnp.bfloat16
F32 = jnp.float32
AXES = {"x": ("c", "x"), "z": ("c", "z"), "y": ("yh", "c", "yl")}
SIZES = {"yh": 2, "c": 2, "x": 4, "z": 4, "yl": 2}
TOK = 384
SLOTS = 128
PAIRS = 82


def shift(value, axis, step):
    pairs = []
    if axis in ("yh", "c", "yl"):
        return lax.ppermute(value, axis, [(0, 1), (1, 0)])
    if axis == "y":
        for yh in range(2):
            for c in range(2):
                for yl in range(2):
                    y = (yh * 2 + yl + (step if c == 0 else -step)) % 4
                    pairs.append(((yh * 2 + c) * 2 + yl, ((y // 2) * 2 + c) * 2 + y % 2))
    else:
        for c in range(2):
            for a in range(4):
                b = (a + (step if c == 0 else -step)) % 4
                pairs.append((c * 4 + a, c * 4 + b))
    return lax.ppermute(value, AXES[axis], pairs)


def add(a, b):
    return (a.astype(F32) + b.astype(F32)).astype(BF)


def sum_of(a, b, c):
    return (a.astype(F32) + b.astype(F32) + c.astype(F32)).astype(BF)


def gates_kernel(gate_ref, up_ref, hid_ref, gu, gut):
    g = gate_ref[...].astype(F32)
    u = up_ref[...].astype(F32)
    h = hid_ref[...].astype(F32)
    sig = 1.0 / (1.0 + jnp.exp(-g))
    gg = h * u * sig * (1.0 + g * (1.0 - sig))
    ug = h * g * sig
    gu[:, :128] = gg.astype(BF)
    gu[:, 128:] = ug.astype(BF)
    gut[:128, :] = gg.T.astype(BF)
    gut[128:, :] = ug.T.astype(BF)


def chunk_kernel(k, tab, order, gu, wg, wu, out):
    @pl.loop(0, 8)
    def _(j):
        base = order[k * 8 + j]
        total = jnp.zeros((TOK, 256), F32)
        for r in range(4):
            sides = []
            for side in range(2):
                slot = tab[r * 64 + base + side]
                index = jnp.minimum(slot, SLOTS - 1)
                block = jnp.concatenate([wg[index], wu[index]], axis=0)
                sides.append(jnp.where(slot < SLOTS, block, jnp.zeros_like(block)))
            both = jnp.concatenate(sides, axis=1)
            total += jnp.dot(gu[:, r * 256 : (r + 1) * 256], both, preferred_element_type=F32)
        out[j] = total.astype(BF)


PIECE = jax.ShapeDtypeStruct((8, TOK, 256), BF)
VM = pl.BlockSpec(memory_space=pltpu.VMEM)
SM = pl.BlockSpec(memory_space=pltpu.SMEM)
ANY = pl.BlockSpec(memory_space=pl.ANY)


def gates(gate_pre, up_pre, hidden):
    return pl.pallas_call(
        gates_kernel,
        out_shape=[jax.ShapeDtypeStruct((TOK, 1024), BF), jax.ShapeDtypeStruct((1024, TOK), BF)],
        grid=(4,),
        in_specs=[pl.BlockSpec((TOK, 128), lambda r: (0, r))] * 3,
        out_specs=[pl.BlockSpec((TOK, 256), lambda r: (0, r)), pl.BlockSpec((256, TOK), lambda r: (r, 0))],
        compiler_params=pltpu.CompilerParams(vmem_limit_bytes=16 * 1024 * 1024),
        cost_estimate=pl.CostEstimate(flops=1, bytes_accessed=1, transcendentals=0),
        name="gates",
    )(gate_pre, up_pre, hidden)


def terms(k, tab, order, gu, wg, wu):
    return pl.pallas_call(
        functools.partial(chunk_kernel, k),
        out_shape=PIECE,
        in_specs=[SM] * 2 + [VM] * 3,
        out_specs=VM,
        compiler_params=pltpu.CompilerParams(vmem_limit_bytes=8 * 1024 * 1024),
        cost_estimate=pl.CostEstimate(flops=1, bytes_accessed=1, transcendentals=0),
        name="terms",
    )(tab, order, gu, wg, wu)


def put(block, grads, slot, sem):
    pltpu.make_async_copy(block, grads.at[slot], sem).start()


def finish(copies, zero, grads, sem):
    @pl.loop(0, copies)
    def _(_):
        pltpu.make_async_copy(zero, grads.at[0], sem).wait()


def same_row_pairs(kind, origin, refs, groups, lrow, lslot, ltile, meta, gt, gate, up, gbuf, ubuf, sem):
    @pl.loop(meta[kind], meta[kind + 1])
    def _(step):
        for pair in range(2):
            pos = step * 4 + pair * 2
            rows = pl.ds(pl.multiple_of(lrow[pos] * 256, 256), 256)
            left = jnp.concatenate([gt[g, rows, :] for g in groups], axis=1)
            sides = []
            for side in range(2):
                tiles = [ref[ltile[(pos + side) * 4 + n]] for n, ref in enumerate(refs)]
                sides.append(jnp.concatenate(tiles, axis=0))
            total = jnp.dot(left, jnp.concatenate(sides, axis=1), preferred_element_type=F32).astype(BF)
            for side in range(2):
                gbuf[pos + side - origin] = total[:128, side * 128 : side * 128 + 128]
                ubuf[pos + side - origin] = total[128:, side * 128 : side * 128 + 128]
        for n in range(4):
            pos = step * 4 + n

            @pl.when(lslot[pos] < SLOTS)
            def _():
                put(gbuf.at[pos - origin], gate, lslot[pos], sem)
                put(ubuf.at[pos - origin], up, lslot[pos], sem)


def kinds_kernel(kinds, held, lrow, lslot, ltile, meta, gt, *rest):
    pieces, (gate, up, gbuf, ubuf, zero, sem) = rest[: len(rest) - 6 - held], rest[-6:]
    origin = meta[kinds[0][0]] * 4
    if not held:
        zero[...] = jnp.zeros((128, 128), BF)

        @pl.loop(meta[8], SLOTS)
        def _(s):
            put(zero, gate, s, sem)
            put(zero, up, s, sem)

        finish(2 * (SLOTS - meta[8]), zero, gate, sem)
    for kind, picks in kinds:
        refs = [pieces[n] for n in picks]
        flip = meta[7]
        groups = (flip, 1 - flip, 3 - flip, 2 + flip) if kind == 3 else (0, 1, 2, 3)
        same_row_pairs(kind, origin, refs, groups, lrow, lslot, ltile, meta, gt, gate, up, gbuf, ubuf, sem)
    finish(2 * (meta[9 + kinds[-1][0] + 1] - meta[9 + kinds[0][0]]), zero, gate, sem)


def weight_grads(name, kinds, room, lists, gt, pieces, held=()):
    grads = jax.ShapeDtypeStruct((SLOTS, 128, 128), BF)
    first = 5 + len(pieces)
    return pl.pallas_call(
        functools.partial(kinds_kernel, kinds, len(held)),
        out_shape=[grads] * 2,
        in_specs=[SM] * 4 + [VM] * (1 + len(pieces)) + [ANY] * len(held),
        out_specs=[ANY] * 2,
        scratch_shapes=[
            pltpu.VMEM((room, 128, 128), BF),
            pltpu.VMEM((room, 128, 128), BF),
            pltpu.VMEM((128, 128), BF),
            pltpu.SemaphoreType.DMA,
        ],
        input_output_aliases={first + n: n for n in range(len(held))},
        compiler_params=pltpu.CompilerParams(vmem_limit_bytes=25 * 1024 * 1024),
        cost_estimate=pl.CostEstimate(flops=1, bytes_accessed=1, transcendentals=0),
        name=name,
    )(*lists, gt, *pieces, *held)


def block_table(block_rows, block_cols, block_count):
    i32 = jnp.int32
    x, z, yl = lax.axis_index("x"), lax.axis_index("z"), lax.axis_index("yl")
    sign = 1 - 2 * lax.axis_index("c")
    slots = jnp.arange(SLOTS, dtype=i32)
    key = jnp.where(slots < block_count[0], block_rows % 4 * 64 + block_cols, -1)
    hit = key[None, :] == jnp.arange(256, dtype=i32)[:, None]
    tab = jnp.min(jnp.where(hit, slots[None, :], SLOTS), axis=1)
    k = jnp.arange(4, dtype=i32)
    xs = (x - sign * k) % 4
    zs = (z - sign * k) % 4
    ys = yl ^ jnp.arange(2, dtype=i32)
    order = (((xs[:, None, None] * 4 + zs[None, :, None]) * 2 + ys[None, None, :]) * 2).reshape(32)
    return tab, order


def slot_lists(block_rows, block_cols, block_count):
    i32 = jnp.int32
    x, z = lax.axis_index("x"), lax.axis_index("z")
    yh, yl = lax.axis_index("yh"), lax.axis_index("yl")
    sign = 1 - 2 * lax.axis_index("c")
    slots = jnp.arange(SLOTS, dtype=i32)
    live = slots < block_count[0]
    row = block_rows % 4
    col = block_cols
    near = (sign * (z - (col >> 2))) % 4
    odd_kind = jnp.where(near == 0, 0, jnp.where(near == 3, 1, jnp.where(near == 1, 2, 5)))
    even_kind = jnp.where(((col >> 1) & 1) == yl, 4, 3)
    kind = jnp.where((col & 1) == 0, even_kind, odd_kind)
    group = kind * 4 + row
    same = (group[:, None] == group[None, :]) & live[None, :]
    rank = jnp.sum(jnp.where(same & (slots[None, :] < slots[:, None]), 1, 0), axis=1)
    groups = jnp.arange(24, dtype=i32)
    count = jnp.sum(jnp.where((group[None, :] == groups[:, None]) & live[None, :], 1, 0), axis=1)
    npair = (count + 1) // 2
    kinds = jnp.arange(6, dtype=i32)
    steps = (jnp.sum(npair.reshape(6, 4), axis=1) + 1) // 2
    edges = jnp.arange(7, dtype=i32)
    before = kinds[None, :] < edges[:, None]
    bounds = jnp.sum(jnp.where(before, steps[None, :], 0), axis=1)
    lives = jnp.sum(jnp.where(before, jnp.sum(count.reshape(6, 4), axis=1)[None, :], 0), axis=1)
    start = jnp.sum(jnp.where(kinds[None, :] < kind[:, None], 2 * steps[None, :], 0), axis=1) + jnp.sum(
        jnp.where((groups[None, :] < group[:, None]) & (groups[None, :] // 4 == kind[:, None]), npair[None, :], 0),
        axis=1,
    )
    place = jnp.where(live, start * 2 + rank, -1)
    at = place[None, :] == jnp.arange(2 * PAIRS, dtype=i32)[:, None]
    lslot = jnp.min(jnp.where(at, slots[None, :], SLOTS), axis=1)
    lrow = jnp.sum(jnp.where(at, row[None, :], 0), axis=1)
    lcol = jnp.sum(jnp.where(at, col[None, :], 0), axis=1)
    cx, cz, cy, par = lcol >> 4, (lcol >> 2) & 3, (lcol >> 1) & 1, lcol & 1
    tiles = []
    for way in (sign, -sign):
        kx = (way * (x - cx)) % 4
        kz = (way * (z - cz)) % 4
        for j in range(2):
            ky = (way * ((yh * 2 + yl) - ((yh ^ j) * 2 + cy))) % 4
            tiles.append(jnp.where(par == 0, kz, ky) * 4 + kx)
    ltile = jnp.stack(tiles, axis=1).reshape(-1)
    flip = jnp.where((yl == 1) == (sign == 1), 0, 1).astype(i32)
    meta = jnp.concatenate([bounds, flip[None], block_count, lives]).astype(i32)
    return lrow, lslot, ltile, meta


def after(value, *others):
    return lax.optimization_barrier((value, *others))[0]


def body(
    activations, gate_pre, up_pre, hidden_grad, gate_blocks, up_blocks, block_rows, block_cols, block_count,
):
    tab, order = block_table(block_rows, block_cols, block_count)
    blocks = (gate_blocks, up_blocks)
    gu, gut = gates(gate_pre, up_pre, hidden_grad)
    other = shift(gut, "yh", 1)
    both = after(jnp.stack([activations[:, :128], activations[:, 128:]]), gut)
    near = [both] + [shift(both, "x", k) for k in (1, 2, 3)]
    t2 = terms(2, tab, order, gu, *blocks)
    ahead = shift(t2, "x", 1)
    even = after(jnp.stack([v[0] for v in near]), t2)
    odd = after(jnp.stack([v[1] for v in near]), t2, other)
    evens, odds = [even], [odd]
    evens.append(shift(even, "z", 1))
    odds.append(shift(odd, "y", 1))
    t1 = terms(1, tab, order, after(gu, even, odd), *blocks)
    back = shift(t1, "x", -1)
    evens.append(shift(after(evens[1], t1), "z", 1))
    odds.append(shift(after(odds[1], t1), "y", 1))
    t3 = terms(3, tab, order, after(gu, evens[1], odds[1]), *blocks)
    evens.append(shift(after(evens[2], t3), "z", 1))
    odds.append(shift(after(odds[2], t3), "y", 1))
    t0 = terms(0, tab, order, after(gu, evens[2], odds[2]), *blocks)
    moving = add(after(ahead, evens[2], odds[2]), t3)
    even_0 = after(jnp.concatenate(evens), t0, moving)
    odd_0 = after(jnp.concatenate(odds), t0, moving)
    even_1, even_3 = shift(even_0, "y", 1), shift(even_0, "y", -1)
    odd_1, odd_3 = shift(odd_0, "z", 1), shift(odd_0, "z", -1)
    ahead = shift(moving, "x", 1)
    rows_late, cols_late, count_late = (after(v, even_0, odd_0) for v in (block_rows, block_cols, block_count))
    lrow, lslot, ltile, meta = slot_lists(rows_late, cols_late, count_late)
    mine = sum_of(t0, ahead, back).reshape(4, 2, TOK, 256)
    own = after(jnp.stack([gut, other]), mine)
    gt = jnp.concatenate([own, shift(own, "c", 1)])
    odd_0c = shift(after(odd_0, mine), "c", 1)

    def grads_of(name, kinds, room, pieces, held=(), wait=()):
        return weight_grads(name, kinds, room, (lrow, lslot, ltile, after(meta, *wait)), gt, pieces, held)

    even_2 = shift(after(even_1, even_3), "y", 1)
    odd_2 = shift(after(odd_1, odd_3), "z", 1)
    odd_1c, odd_3c = shift(odd_1, "c", 1), shift(odd_3, "c", 1)
    even_1c, even_3c = (shift(after(v, odd_1c, odd_3c, odd_0c), "c", 1) for v in (even_1, even_3))
    grads = grads_of(
        "grads_0_1_2",
        ((0, (0, 0, 1, 1)), (1, (3, 3, 4, 4)), (2, (2, 2, 5, 5))),
        116,
        (odd_0, odd_0c, odd_1, odd_3, odd_1c, odd_3c),
    )
    even_0c = shift(after(even_0, grads[0]), "c", 1)
    even_2 = after(even_2, grads[0])
    ahead = shift(after(mine[2], grads[0]), "z", 1)
    back = shift(after(mine[1], grads[0]), "z", -1)
    grads = grads_of("grads_3", ((3, (0, 1, 2, 3)),), 72, (even_1, even_3, even_1c, even_3c), grads, (even_2,))
    even_2c = shift(even_2, "c", 1)
    odd_2c = shift(odd_2, "c", 1)
    ahead = add(after(ahead, grads[0]), mine[3])
    grads = grads_of(
        "grads_4", ((4, (0, 1, 2, 3)),), 72, (even_0, even_2, even_0c, even_2c), grads, (ahead, odd_2)
    )
    ahead = after(shift(ahead, "z", 1), grads[0])
    send = sum_of(mine[0, 1], ahead[1], back[1])
    keep = mine[0, 0].astype(F32) + ahead[0].astype(F32) + back[0].astype(F32)
    gate_grad, up_grad = grads_of("grads_5", ((5, (0, 0, 1, 1)),), 40, (odd_2, odd_2c), grads, (send,))
    input_grad = (keep + after(shift(send, "yl", 1), gate_grad).astype(F32)).astype(BF)
    return input_grad, gate_grad, up_grad


def solution(mesh):
    fine = Mesh(mesh.devices.reshape(2, 2, 4, 4, 2), ("yh", "c", "x", "z", "yl"))
    tok, wt = ("yh", "c"), ("x", "z", "yl")
    in_specs = (P(tok, wt),) * 4 + (P(wt, None, None),) * 2 + (P(wt),) * 3
    out_specs = (P(tok, wt), P(wt, None, None), P(wt, None, None))
    return jax.shard_map(body, mesh=fine, in_specs=in_specs, out_specs=out_specs, check_vma=False)
```

```python
import functools

import jax
import jax.numpy as jnp
from jax import lax
from jax.experimental import pallas as pl
from jax.experimental.pallas import tpu as pltpu
from jax.sharding import Mesh
from jax.sharding import PartitionSpec as P

BF = jnp.bfloat16
F32 = jnp.float32
AXES = {"x": ("c", "x"), "z": ("c", "z"), "y": ("yh", "c", "yl")}
SIZES = {"yh": 2, "c": 2, "x": 4, "z": 4, "yl": 2}
TOK = 384
SLOTS = 128
PAIRS = 82


def shift(value, axis, step):
    pairs = []
    if axis in ("yh", "c", "yl"):
        return lax.ppermute(value, axis, [(0, 1), (1, 0)])
    if axis == "y":
        for yh in range(2):
            for c in range(2):
                for yl in range(2):
                    y = (yh * 2 + yl + (step if c == 0 else -step)) % 4
                    pairs.append(((yh * 2 + c) * 2 + yl, ((y // 2) * 2 + c) * 2 + y % 2))
    else:
        for c in range(2):
            for a in range(4):
                b = (a + (step if c == 0 else -step)) % 4
                pairs.append((c * 4 + a, c * 4 + b))
    return lax.ppermute(value, AXES[axis], pairs)


def add(a, b):
    return (a.astype(F32) + b.astype(F32)).astype(BF)


def sum_of(a, b, c):
    return (a.astype(F32) + b.astype(F32) + c.astype(F32)).astype(BF)


def gates_kernel(gate_ref, up_ref, hid_ref, gu, gut):
    g = gate_ref[...].astype(F32)
    u = up_ref[...].astype(F32)
    h = hid_ref[...].astype(F32)
    sig = 1.0 / (1.0 + jnp.exp(-g))
    gg = h * u * sig * (1.0 + g * (1.0 - sig))
    ug = h * g * sig
    gu[:, :128] = gg.astype(BF)
    gu[:, 128:] = ug.astype(BF)
    gut[:128, :] = gg.T.astype(BF)
    gut[128:, :] = ug.T.astype(BF)


def chunk_kernel(chunks, tab, order, gu, wg, wu, *outs):
    for k, out in zip(chunks, outs):

        @pl.loop(0, 8)
        def _(j):
            base = order[k * 8 + j]
            total = jnp.zeros((TOK, 256), F32)
            for r in range(4):
                sides = []
                for side in range(2):
                    slot = tab[r * 64 + base + side]
                    index = jnp.minimum(slot, SLOTS - 1)
                    block = jnp.concatenate([wg[index], wu[index]], axis=0)
                    sides.append(jnp.where(slot < SLOTS, block, jnp.zeros_like(block)))
                both = jnp.concatenate(sides, axis=1)
                total += jnp.dot(gu[:, r * 256 : (r + 1) * 256], both, preferred_element_type=F32)
            out[j] = total.astype(BF)


PIECE = jax.ShapeDtypeStruct((8, TOK, 256), BF)
VM = pl.BlockSpec(memory_space=pltpu.VMEM)
SM = pl.BlockSpec(memory_space=pltpu.SMEM)
ANY = pl.BlockSpec(memory_space=pl.ANY)


def gates(gate_pre, up_pre, hidden):
    return pl.pallas_call(
        gates_kernel,
        out_shape=[jax.ShapeDtypeStruct((TOK, 1024), BF), jax.ShapeDtypeStruct((1024, TOK), BF)],
        grid=(4,),
        in_specs=[pl.BlockSpec((TOK, 128), lambda r: (0, r))] * 3,
        out_specs=[pl.BlockSpec((TOK, 256), lambda r: (0, r)), pl.BlockSpec((256, TOK), lambda r: (r, 0))],
        compiler_params=pltpu.CompilerParams(vmem_limit_bytes=16 * 1024 * 1024),
        cost_estimate=pl.CostEstimate(flops=1, bytes_accessed=1, transcendentals=0),
        name="gates",
    )(gate_pre, up_pre, hidden)


def terms(chunks, tab, order, gu, wg, wu):
    return pl.pallas_call(
        functools.partial(chunk_kernel, chunks),
        out_shape=[PIECE] * len(chunks),
        in_specs=[SM] * 2 + [VM] * 3,
        out_specs=[VM] * len(chunks),
        compiler_params=pltpu.CompilerParams(vmem_limit_bytes=8 * 1024 * 1024),
        cost_estimate=pl.CostEstimate(flops=1, bytes_accessed=1, transcendentals=0),
        name="terms",
    )(tab, order, gu, wg, wu)


def put(block, grads, slot, sem):
    pltpu.make_async_copy(block, grads.at[slot], sem).start()


def finish(copies, zero, grads, sem):
    @pl.loop(0, copies)
    def _(_):
        pltpu.make_async_copy(zero, grads.at[0], sem).wait()


def same_row_pairs(kind, origin, refs, groups, lrow, lslot, ltile, meta, gt, gate, up, gbuf, ubuf, sem):
    @pl.loop(meta[kind], meta[kind + 1])
    def _(step):
        for pair in range(2):
            pos = step * 4 + pair * 2
            rows = pl.ds(pl.multiple_of(lrow[pos] * 256, 256), 256)
            left = jnp.concatenate([gt[g, rows, :] for g in groups], axis=1)
            sides = []
            for side in range(2):
                tiles = [ref[ltile[(pos + side) * 4 + n]] for n, ref in enumerate(refs)]
                sides.append(jnp.concatenate(tiles, axis=0))
            total = jnp.dot(left, jnp.concatenate(sides, axis=1), preferred_element_type=F32).astype(BF)
            for side in range(2):
                gbuf[pos + side - origin] = total[:128, side * 128 : side * 128 + 128]
                ubuf[pos + side - origin] = total[128:, side * 128 : side * 128 + 128]
        for n in range(4):
            pos = step * 4 + n

            @pl.when(lslot[pos] < SLOTS)
            def _():
                put(gbuf.at[pos - origin], gate, lslot[pos], sem)
                put(ubuf.at[pos - origin], up, lslot[pos], sem)


def kinds_kernel(kinds, held, lrow, lslot, ltile, meta, gt, *rest):
    pieces, (gate, up, gbuf, ubuf, zero, sem) = rest[: len(rest) - 6 - held], rest[-6:]
    origin = meta[kinds[0][0]] * 4
    if not held:
        zero[...] = jnp.zeros((128, 128), BF)

        @pl.loop(meta[8], SLOTS)
        def _(s):
            put(zero, gate, s, sem)
            put(zero, up, s, sem)

        finish(2 * (SLOTS - meta[8]), zero, gate, sem)
    for kind, picks in kinds:
        refs = [pieces[n] for n in picks]
        flip = meta[7]
        groups = (flip, 1 - flip, 3 - flip, 2 + flip) if kind == 3 else (0, 1, 2, 3)
        same_row_pairs(kind, origin, refs, groups, lrow, lslot, ltile, meta, gt, gate, up, gbuf, ubuf, sem)
    finish(2 * (meta[9 + kinds[-1][0] + 1] - meta[9 + kinds[0][0]]), zero, gate, sem)


def weight_grads(name, kinds, room, lists, gt, pieces, held=()):
    grads = jax.ShapeDtypeStruct((SLOTS, 128, 128), BF)
    first = 5 + len(pieces)
    return pl.pallas_call(
        functools.partial(kinds_kernel, kinds, len(held)),
        out_shape=[grads] * 2,
        in_specs=[SM] * 4 + [VM] * (1 + len(pieces)) + [ANY] * len(held),
        out_specs=[ANY] * 2,
        scratch_shapes=[
            pltpu.VMEM((room, 128, 128), BF),
            pltpu.VMEM((room, 128, 128), BF),
            pltpu.VMEM((128, 128), BF),
            pltpu.SemaphoreType.DMA,
        ],
        input_output_aliases={first + n: n for n in range(len(held))},
        compiler_params=pltpu.CompilerParams(vmem_limit_bytes=13 * 1024 * 1024),
        cost_estimate=pl.CostEstimate(flops=1, bytes_accessed=1, transcendentals=0),
        name=name,
    )(*lists, gt, *pieces, *held)


def block_table(block_rows, block_cols, block_count):
    i32 = jnp.int32
    x, z, yl = lax.axis_index("x"), lax.axis_index("z"), lax.axis_index("yl")
    sign = 1 - 2 * lax.axis_index("c")
    slots = jnp.arange(SLOTS, dtype=i32)
    key = jnp.where(slots < block_count[0], block_rows % 4 * 64 + block_cols, -1)
    hit = key[None, :] == jnp.arange(256, dtype=i32)[:, None]
    tab = jnp.min(jnp.where(hit, slots[None, :], SLOTS), axis=1)
    k = jnp.arange(4, dtype=i32)
    xs = (x - sign * k) % 4
    zs = (z - sign * k) % 4
    ys = yl ^ jnp.arange(2, dtype=i32)
    order = (((xs[:, None, None] * 4 + zs[None, :, None]) * 2 + ys[None, None, :]) * 2).reshape(32)
    return tab, order


def slot_lists(block_rows, block_cols, block_count):
    i32 = jnp.int32
    x, z = lax.axis_index("x"), lax.axis_index("z")
    yh, yl = lax.axis_index("yh"), lax.axis_index("yl")
    sign = 1 - 2 * lax.axis_index("c")
    slots = jnp.arange(SLOTS, dtype=i32)
    live = slots < block_count[0]
    row = block_rows % 4
    col = block_cols
    near = (sign * (z - (col >> 2))) % 4
    odd_kind = jnp.where(near == 0, 0, jnp.where(near == 3, 1, jnp.where(near == 1, 2, 5)))
    even_kind = jnp.where(((col >> 1) & 1) == yl, 4, 3)
    kind = jnp.where((col & 1) == 0, even_kind, odd_kind)
    group = kind * 4 + row
    same = (group[:, None] == group[None, :]) & live[None, :]
    rank = jnp.sum(jnp.where(same & (slots[None, :] < slots[:, None]), 1, 0), axis=1)
    groups = jnp.arange(24, dtype=i32)
    count = jnp.sum(jnp.where((group[None, :] == groups[:, None]) & live[None, :], 1, 0), axis=1)
    npair = (count + 1) // 2
    kinds = jnp.arange(6, dtype=i32)
    steps = (jnp.sum(npair.reshape(6, 4), axis=1) + 1) // 2
    edges = jnp.arange(7, dtype=i32)
    before = kinds[None, :] < edges[:, None]
    bounds = jnp.sum(jnp.where(before, steps[None, :], 0), axis=1)
    lives = jnp.sum(jnp.where(before, jnp.sum(count.reshape(6, 4), axis=1)[None, :], 0), axis=1)
    start = jnp.sum(jnp.where(kinds[None, :] < kind[:, None], 2 * steps[None, :], 0), axis=1) + jnp.sum(
        jnp.where((groups[None, :] < group[:, None]) & (groups[None, :] // 4 == kind[:, None]), npair[None, :], 0),
        axis=1,
    )
    place = jnp.where(live, start * 2 + rank, -1)
    at = place[None, :] == jnp.arange(2 * PAIRS, dtype=i32)[:, None]
    lslot = jnp.min(jnp.where(at, slots[None, :], SLOTS), axis=1)
    lrow = jnp.sum(jnp.where(at, row[None, :], 0), axis=1)
    lcol = jnp.sum(jnp.where(at, col[None, :], 0), axis=1)
    cx, cz, cy, par = lcol >> 4, (lcol >> 2) & 3, (lcol >> 1) & 1, lcol & 1
    tiles = []
    for way in (sign, -sign):
        kx = (way * (x - cx)) % 4
        kz = (way * (z - cz)) % 4
        for j in range(2):
            ky = (way * ((yh * 2 + yl) - ((yh ^ j) * 2 + cy))) % 4
            tiles.append(jnp.where(par == 0, kz, ky) * 4 + kx)
    ltile = jnp.stack(tiles, axis=1).reshape(-1)
    flip = jnp.where((yl == 1) == (sign == 1), 0, 1).astype(i32)
    meta = jnp.concatenate([bounds, flip[None], block_count, lives]).astype(i32)
    return lrow, lslot, ltile, meta


def after(value, *others):
    return lax.optimization_barrier((value, *others))[0]


def body(
    activations, gate_pre, up_pre, hidden_grad, gate_blocks, up_blocks, block_rows, block_cols, block_count,
):
    tab, order = block_table(block_rows, block_cols, block_count)
    blocks = (gate_blocks, up_blocks)
    gu, gut = gates(gate_pre, up_pre, hidden_grad)
    other = shift(gut, "yh", 1)
    both = after(jnp.stack([activations[:, :128], activations[:, 128:]]), gut)
    near = [both] + [shift(both, "x", k) for k in (1, 2, 3)]
    (t2,) = terms((2,), tab, order, gu, *blocks)
    ahead = shift(t2, "x", 1)
    even = after(jnp.stack([v[0] for v in near]), t2)
    odd = after(jnp.stack([v[1] for v in near]), t2, other)
    evens, odds = [even], [odd]
    evens.append(shift(even, "z", 1))
    odds.append(shift(odd, "y", 1))
    (t1,) = terms((1,), tab, order, after(gu, even, odd), *blocks)
    back = shift(t1, "x", -1)
    evens.append(shift(after(evens[1], t1), "z", 1))
    odds.append(shift(after(odds[1], t1), "y", 1))
    t3, t0 = terms((3, 0), tab, order, after(gu, evens[1], odds[1]), *blocks)
    evens.append(shift(after(evens[2], t3), "z", 1))
    odds.append(shift(after(odds[2], t3), "y", 1))
    moving = add(after(ahead, evens[2], odds[2]), t3)
    even_0 = after(jnp.concatenate(evens), t0, moving)
    odd_0 = after(jnp.concatenate(odds), t0, moving)
    even_1, even_3 = shift(even_0, "y", 1), shift(even_0, "y", -1)
    odd_1, odd_3 = shift(odd_0, "z", 1), shift(odd_0, "z", -1)
    ahead = shift(moving, "x", 1)
    rows_late, cols_late, count_late = (after(v, even_0, odd_0) for v in (block_rows, block_cols, block_count))
    lrow, lslot, ltile, meta = slot_lists(rows_late, cols_late, count_late)
    mine = sum_of(t0, ahead, back).reshape(4, 2, TOK, 256)
    own = after(jnp.stack([gut, other]), mine)
    gt = jnp.concatenate([own, shift(own, "c", 1)])
    odd_0c = shift(after(odd_0, mine), "c", 1)

    def grads_of(name, kinds, room, pieces, held=(), wait=()):
        return weight_grads(name, kinds, room, (lrow, lslot, ltile, after(meta, *wait)), gt, pieces, held)

    even_2 = shift(after(even_1, even_3), "y", 1)
    odd_2 = shift(after(odd_1, odd_3), "z", 1)
    odd_1c, odd_3c = shift(odd_1, "c", 1), shift(odd_3, "c", 1)
    even_1c, even_3c = (shift(after(v, odd_1c, odd_3c, odd_0c), "c", 1) for v in (even_1, even_3))
    grads = grads_of("grads_0", ((0, (0, 0, 1, 1)),), 40, (odd_0, odd_0c))
    grads = grads_of("grads_1", ((1, (0, 0, 1, 1)),), 40, (odd_3, odd_1c), grads)
    grads = grads_of("grads_2", ((2, (0, 0, 1, 1)),), 40, (odd_1, odd_3c), grads)
    even_0c = shift(after(even_0, grads[0]), "c", 1)
    even_2 = after(even_2, grads[0])
    ahead = shift(after(mine[2], odd_3c), "z", 1)
    back = shift(after(mine[1], odd_3c), "z", -1)
    grads = grads_of("grads_3", ((3, (0, 1, 2, 3)),), 72, (even_1, even_3, even_1c, even_3c), grads, (even_2,))
    even_2c = shift(even_2, "c", 1)
    odd_2c = shift(odd_2, "c", 1)
    ahead = add(after(ahead, grads[0]), mine[3])
    grads = grads_of(
        "grads_4", ((4, (0, 1, 2, 3)),), 72, (even_0, even_2, even_0c, even_2c), grads, (ahead, odd_2)
    )
    ahead = after(shift(ahead, "z", 1), grads[0])
    send = sum_of(mine[0, 1], ahead[1], back[1])
    keep = mine[0, 0].astype(F32) + ahead[0].astype(F32) + back[0].astype(F32)
    gate_grad, up_grad = grads_of("grads_5", ((5, (0, 0, 1, 1)),), 40, (odd_2, odd_2c), grads, (send,))
    input_grad = (keep + after(shift(send, "yl", 1), gate_grad).astype(F32)).astype(BF)
    return input_grad, gate_grad, up_grad


def solution(mesh):
    fine = Mesh(mesh.devices.reshape(2, 2, 4, 4, 2), ("yh", "c", "x", "z", "yl"))
    tok, wt = ("yh", "c"), ("x", "z", "yl")
    in_specs = (P(tok, wt),) * 4 + (P(wt, None, None),) * 2 + (P(wt),) * 3
    out_specs = (P(tok, wt), P(wt, None, None), P(wt, None, None))
    return jax.shard_map(body, mesh=fine, in_specs=in_specs, out_specs=out_specs, check_vma=False)
```

```python
import functools

import jax
import jax.numpy as jnp
from jax import lax
from jax.experimental import pallas as pl
from jax.experimental.pallas import tpu as pltpu
from jax.sharding import Mesh
from jax.sharding import PartitionSpec as P

BF = jnp.bfloat16
F32 = jnp.float32
AXES = {"x": ("c", "x"), "z": ("c", "z"), "y": ("yh", "c", "yl")}
SIZES = {"yh": 2, "c": 2, "x": 4, "z": 4, "yl": 2}
TOK = 384
SLOTS = 128
PAIRS = 82


def shift(value, axis, step):
    pairs = []
    if axis in ("yh", "c", "yl"):
        return lax.ppermute(value, axis, [(0, 1), (1, 0)])
    if axis == "y":
        for yh in range(2):
            for c in range(2):
                for yl in range(2):
                    y = (yh * 2 + yl + (step if c == 0 else -step)) % 4
                    pairs.append(((yh * 2 + c) * 2 + yl, ((y // 2) * 2 + c) * 2 + y % 2))
    else:
        for c in range(2):
            for a in range(4):
                b = (a + (step if c == 0 else -step)) % 4
                pairs.append((c * 4 + a, c * 4 + b))
    return lax.ppermute(value, AXES[axis], pairs)


def add(a, b):
    return (a.astype(F32) + b.astype(F32)).astype(BF)


def sum_of(a, b, c):
    return (a.astype(F32) + b.astype(F32) + c.astype(F32)).astype(BF)


def gates_kernel(gate_ref, up_ref, hid_ref, gu, gut):
    g = gate_ref[...].astype(F32)
    u = up_ref[...].astype(F32)
    h = hid_ref[...].astype(F32)
    sig = 1.0 / (1.0 + jnp.exp(-g))
    gg = h * u * sig * (1.0 + g * (1.0 - sig))
    ug = h * g * sig
    gu[:, :128] = gg.astype(BF)
    gu[:, 128:] = ug.astype(BF)
    gut[:128, :] = gg.T.astype(BF)
    gut[128:, :] = ug.T.astype(BF)


def chunk_kernel(chunks, tab, order, gu, wg, wu, *outs):
    for k, out in zip(chunks, outs):

        @pl.loop(0, 8)
        def _(j):
            base = order[k * 8 + j]
            total = jnp.zeros((TOK, 256), F32)
            for r in range(4):
                sides = []
                for side in range(2):
                    slot = tab[r * 64 + base + side]
                    index = jnp.minimum(slot, SLOTS - 1)
                    block = jnp.concatenate([wg[index], wu[index]], axis=0)
                    sides.append(jnp.where(slot < SLOTS, block, jnp.zeros_like(block)))
                both = jnp.concatenate(sides, axis=1)
                total += jnp.dot(gu[:, r * 256 : (r + 1) * 256], both, preferred_element_type=F32)
            out[j] = total.astype(BF)


PIECE = jax.ShapeDtypeStruct((8, TOK, 256), BF)
VM = pl.BlockSpec(memory_space=pltpu.VMEM)
SM = pl.BlockSpec(memory_space=pltpu.SMEM)
ANY = pl.BlockSpec(memory_space=pl.ANY)


def gates(gate_pre, up_pre, hidden):
    return pl.pallas_call(
        gates_kernel,
        out_shape=[jax.ShapeDtypeStruct((TOK, 1024), BF), jax.ShapeDtypeStruct((1024, TOK), BF)],
        grid=(4,),
        in_specs=[pl.BlockSpec((TOK, 128), lambda r: (0, r))] * 3,
        out_specs=[pl.BlockSpec((TOK, 256), lambda r: (0, r)), pl.BlockSpec((256, TOK), lambda r: (r, 0))],
        compiler_params=pltpu.CompilerParams(vmem_limit_bytes=16 * 1024 * 1024),
        cost_estimate=pl.CostEstimate(flops=1, bytes_accessed=1, transcendentals=0),
        name="gates",
    )(gate_pre, up_pre, hidden)


def terms(chunks, tab, order, gu, wg, wu):
    return pl.pallas_call(
        functools.partial(chunk_kernel, chunks),
        out_shape=[PIECE] * len(chunks),
        in_specs=[SM] * 2 + [VM] * 3,
        out_specs=[VM] * len(chunks),
        compiler_params=pltpu.CompilerParams(vmem_limit_bytes=8 * 1024 * 1024),
        cost_estimate=pl.CostEstimate(flops=1, bytes_accessed=1, transcendentals=0),
        name="terms",
    )(tab, order, gu, wg, wu)


def put(block, grads, slot, sem):
    pltpu.make_async_copy(block, grads.at[slot], sem).start()


def finish(copies, zero, grads, sem):
    @pl.loop(0, copies)
    def _(_):
        pltpu.make_async_copy(zero, grads.at[0], sem).wait()


def same_row_pairs(kind, origin, refs, groups, lrow, lslot, ltile, meta, gts, gate, up, gbuf, ubuf, sem):
    @pl.loop(meta[kind], meta[kind + 1])
    def _(step):
        for pair in range(2):
            pos = step * 4 + pair * 2
            rows = pl.ds(pl.multiple_of(lrow[pos] * 256, 256), 256)
            left = jnp.concatenate([gts[n // 2][g, rows, :] for n, g in enumerate(groups)], axis=1)
            sides = []
            for side in range(2):
                tiles = [ref[ltile[(pos + side) * 4 + n]] for n, ref in enumerate(refs)]
                sides.append(jnp.concatenate(tiles, axis=0))
            total = jnp.dot(left, jnp.concatenate(sides, axis=1), preferred_element_type=F32).astype(BF)
            for side in range(2):
                gbuf[pos + side - origin] = total[:128, side * 128 : side * 128 + 128]
                ubuf[pos + side - origin] = total[128:, side * 128 : side * 128 + 128]
        for n in range(4):
            pos = step * 4 + n

            @pl.when(lslot[pos] < SLOTS)
            def _():
                put(gbuf.at[pos - origin], gate, lslot[pos], sem)
                put(ubuf.at[pos - origin], up, lslot[pos], sem)


def kinds_kernel(kinds, held, lrow, lslot, ltile, meta, gt, gt_c, *rest):
    pieces, (gate, up, gbuf, ubuf, zero, sem) = rest[: len(rest) - 6 - held], rest[-6:]
    origin = meta[kinds[0][0]] * 4
    if not held:
        zero[...] = jnp.zeros((128, 128), BF)

        @pl.loop(meta[8], SLOTS)
        def _(s):
            put(zero, gate, s, sem)
            put(zero, up, s, sem)

        finish(2 * (SLOTS - meta[8]), zero, gate, sem)
    for kind, picks in kinds:
        refs = [pieces[n] for n in picks]
        flip = meta[7]
        groups = (flip, 1 - flip, 1 - flip, flip) if kind == 3 else (0, 1, 0, 1)
        same_row_pairs(kind, origin, refs, groups, lrow, lslot, ltile, meta, (gt, gt_c), gate, up, gbuf, ubuf, sem)
    finish(2 * (meta[9 + kinds[-1][0] + 1] - meta[9 + kinds[0][0]]), zero, gate, sem)


def weight_grads(name, kinds, room, lists, gts, pieces, held=()):
    grads = jax.ShapeDtypeStruct((SLOTS, 128, 128), BF)
    first = 6 + len(pieces)
    return pl.pallas_call(
        functools.partial(kinds_kernel, kinds, len(held)),
        out_shape=[grads] * 2,
        in_specs=[SM] * 4 + [VM] * (2 + len(pieces)) + [ANY] * len(held),
        out_specs=[ANY] * 2,
        scratch_shapes=[
            pltpu.VMEM((room, 128, 128), BF),
            pltpu.VMEM((room, 128, 128), BF),
            pltpu.VMEM((128, 128), BF),
            pltpu.SemaphoreType.DMA,
        ],
        input_output_aliases={first + n: n for n in range(len(held))},
        compiler_params=pltpu.CompilerParams(vmem_limit_bytes=13 * 1024 * 1024),
        cost_estimate=pl.CostEstimate(flops=1, bytes_accessed=1, transcendentals=0),
        name=name,
    )(*lists, *gts, *pieces, *held)


def block_table(block_rows, block_cols, block_count):
    i32 = jnp.int32
    x, z, yl = lax.axis_index("x"), lax.axis_index("z"), lax.axis_index("yl")
    sign = 1 - 2 * lax.axis_index("c")
    slots = jnp.arange(SLOTS, dtype=i32)
    key = jnp.where(slots < block_count[0], block_rows % 4 * 64 + block_cols, -1)
    hit = key[None, :] == jnp.arange(256, dtype=i32)[:, None]
    tab = jnp.min(jnp.where(hit, slots[None, :], SLOTS), axis=1)
    k = jnp.arange(4, dtype=i32)
    xs = (x - sign * k) % 4
    zs = (z - sign * k) % 4
    ys = yl ^ jnp.arange(2, dtype=i32)
    order = (((xs[:, None, None] * 4 + zs[None, :, None]) * 2 + ys[None, None, :]) * 2).reshape(32)
    return tab, order


def slot_lists(block_rows, block_cols, block_count):
    i32 = jnp.int32
    x, z = lax.axis_index("x"), lax.axis_index("z")
    yh, yl = lax.axis_index("yh"), lax.axis_index("yl")
    sign = 1 - 2 * lax.axis_index("c")
    slots = jnp.arange(SLOTS, dtype=i32)
    live = slots < block_count[0]
    row = block_rows % 4
    col = block_cols
    near = (sign * (z - (col >> 2))) % 4
    odd_kind = jnp.where(near == 0, 0, jnp.where(near == 3, 1, jnp.where(near == 1, 2, 5)))
    even_kind = jnp.where(((col >> 1) & 1) == yl, 4, 3)
    kind = jnp.where((col & 1) == 0, even_kind, odd_kind)
    group = kind * 4 + row
    same = (group[:, None] == group[None, :]) & live[None, :]
    rank = jnp.sum(jnp.where(same & (slots[None, :] < slots[:, None]), 1, 0), axis=1)
    groups = jnp.arange(24, dtype=i32)
    count = jnp.sum(jnp.where((group[None, :] == groups[:, None]) & live[None, :], 1, 0), axis=1)
    npair = (count + 1) // 2
    kinds = jnp.arange(6, dtype=i32)
    steps = (jnp.sum(npair.reshape(6, 4), axis=1) + 1) // 2
    edges = jnp.arange(7, dtype=i32)
    before = kinds[None, :] < edges[:, None]
    bounds = jnp.sum(jnp.where(before, steps[None, :], 0), axis=1)
    lives = jnp.sum(jnp.where(before, jnp.sum(count.reshape(6, 4), axis=1)[None, :], 0), axis=1)
    start = jnp.sum(jnp.where(kinds[None, :] < kind[:, None], 2 * steps[None, :], 0), axis=1) + jnp.sum(
        jnp.where((groups[None, :] < group[:, None]) & (groups[None, :] // 4 == kind[:, None]), npair[None, :], 0),
        axis=1,
    )
    place = jnp.where(live, start * 2 + rank, -1)
    at = place[None, :] == jnp.arange(2 * PAIRS, dtype=i32)[:, None]
    lslot = jnp.min(jnp.where(at, slots[None, :], SLOTS), axis=1)
    lrow = jnp.sum(jnp.where(at, row[None, :], 0), axis=1)
    lcol = jnp.sum(jnp.where(at, col[None, :], 0), axis=1)
    cx, cz, cy, par = lcol >> 4, (lcol >> 2) & 3, (lcol >> 1) & 1, lcol & 1
    tiles = []
    for way in (sign, -sign):
        kx = (way * (x - cx)) % 4
        kz = (way * (z - cz)) % 4
        for j in range(2):
            ky = (way * ((yh * 2 + yl) - ((yh ^ j) * 2 + cy))) % 4
            tiles.append(jnp.where(par == 0, kz, ky) * 4 + kx)
    ltile = jnp.stack(tiles, axis=1).reshape(-1)
    flip = jnp.where((yl == 1) == (sign == 1), 0, 1).astype(i32)
    meta = jnp.concatenate([bounds, flip[None], block_count, lives]).astype(i32)
    return lrow, lslot, ltile, meta


def after(value, *others):
    return lax.optimization_barrier((value, *others))[0]


def body(
    activations, gate_pre, up_pre, hidden_grad, gate_blocks, up_blocks, block_rows, block_cols, block_count,
):
    tab, order = block_table(block_rows, block_cols, block_count)
    blocks = (gate_blocks, up_blocks)
    gu, gut = gates(gate_pre, up_pre, hidden_grad)
    other = shift(gut, "yh", 1)
    both = after(jnp.stack([activations[:, :128], activations[:, 128:]]), gut)
    near = [both] + [shift(both, "x", k) for k in (1, 2, 3)]
    (t2,) = terms((2,), tab, order, gu, *blocks)
    ahead = shift(t2, "x", 1)
    even = after(jnp.stack([v[0] for v in near]), t2)
    odd = after(jnp.stack([v[1] for v in near]), t2, other)
    evens, odds = [even], [odd]
    evens.append(shift(even, "z", 1))
    odds.append(shift(odd, "y", 1))
    (t1,) = terms((1,), tab, order, after(gu, even, odd), *blocks)
    back = shift(t1, "x", -1)
    evens.append(shift(after(evens[1], t1), "z", 1))
    odds.append(shift(after(odds[1], t1), "y", 1))
    t3, t0 = terms((3, 0), tab, order, after(gu, evens[1], odds[1]), *blocks)
    evens.append(shift(after(evens[2], t3), "z", 1))
    odds.append(shift(after(odds[2], t3), "y", 1))
    moving = add(after(ahead, evens[2], odds[2]), t3)
    even_0 = after(jnp.concatenate(evens), t0, moving)
    odd_0 = after(jnp.concatenate(odds), t0, moving)
    even_1, even_3 = shift(even_0, "y", 1), shift(even_0, "y", -1)
    odd_1, odd_3 = shift(odd_0, "z", 1), shift(odd_0, "z", -1)
    ahead = shift(moving, "x", 1)
    rows_late, cols_late, count_late = (after(v, even_0, odd_0) for v in (block_rows, block_cols, block_count))
    lrow, lslot, ltile, meta = slot_lists(rows_late, cols_late, count_late)
    mine = sum_of(t0, ahead, back).reshape(4, 2, TOK, 256)
    own = jnp.stack([gut, other])
    own_c = shift(own, "c", 1)
    odd_0c = shift(after(odd_0, mine, own_c), "c", 1)

    def grads_of(name, kinds, room, pieces, held=(), wait=()):
        return weight_grads(name, kinds, room, (lrow, lslot, ltile, after(meta, *wait)), (own, own_c), pieces, held)

    even_2 = shift(after(even_1, even_3), "y", 1)
    odd_2 = shift(after(odd_1, odd_3), "z", 1)
    odd_1c, odd_3c = shift(odd_1, "c", 1), shift(odd_3, "c", 1)
    even_1c, even_3c = (shift(after(v, odd_1c, odd_3c, odd_0c), "c", 1) for v in (even_1, even_3))
    ahead = shift(after(mine[2], odd_3c), "z", 1)
    back = shift(after(mine[1], odd_3c), "z", -1)
    ahead = add(ahead, mine[3])
    grads = grads_of("grads_0", ((0, (0, 0, 1, 1)),), 40, (odd_0, odd_0c))
    grads = grads_of("grads_1", ((1, (0, 0, 1, 1)),), 40, (odd_3, odd_1c), grads)
    grads = grads_of("grads_2", ((2, (0, 0, 1, 1)),), 40, (odd_1, odd_3c), grads, (ahead,))
    ahead = shift(ahead, "z", 1)
    even_0c = shift(after(even_0, grads[0]), "c", 1)
    even_2 = after(even_2, grads[0])
    grads = grads_of("grads_3", ((3, (0, 1, 2, 3)),), 72, (even_1, even_3, even_1c, even_3c), grads, (even_2, back))
    even_2c = shift(even_2, "c", 1)
    odd_2c = shift(odd_2, "c", 1)
    ahead = after(ahead, grads[0])
    send = sum_of(mine[0, 1], ahead[1], back[1])
    keep = mine[0, 0].astype(F32) + ahead[0].astype(F32) + back[0].astype(F32)
    grads = grads_of(
        "grads_4", ((4, (0, 1, 2, 3)),), 72, (even_0, even_2, even_0c, even_2c), grads, (send, odd_2)
    )
    gate_grad, up_grad = grads_of("grads_5", ((5, (0, 0, 1, 1)),), 40, (odd_2, odd_2c), grads)
    input_grad = (keep + after(shift(send, "yl", 1), grads[0]).astype(F32)).astype(BF)
    return input_grad, gate_grad, up_grad


def solution(mesh):
    fine = Mesh(mesh.devices.reshape(2, 2, 4, 4, 2), ("yh", "c", "x", "z", "yl"))
    tok, wt = ("yh", "c"), ("x", "z", "yl")
    in_specs = (P(tok, wt),) * 4 + (P(wt, None, None),) * 2 + (P(wt),) * 3
    out_specs = (P(tok, wt), P(wt, None, None), P(wt, None, None))
    return jax.shard_map(body, mesh=fine, in_specs=in_specs, out_specs=out_specs, check_vma=False)
```

```python
import functools

import jax
import jax.numpy as jnp
from jax import lax
from jax.experimental import pallas as pl
from jax.experimental.pallas import tpu as pltpu
from jax.sharding import Mesh
from jax.sharding import PartitionSpec as P

BF = jnp.bfloat16
F32 = jnp.float32
AXES = {"x": ("c", "x"), "z": ("c", "z"), "y": ("yh", "c", "yl")}
SIZES = {"yh": 2, "c": 2, "x": 4, "z": 4, "yl": 2}
TOK = 384
SLOTS = 128
PAIRS = 82


def shift(value, axis, step):
    pairs = []
    if axis in ("yh", "c", "yl"):
        return lax.ppermute(value, axis, [(0, 1), (1, 0)])
    if axis == "y":
        for yh in range(2):
            for c in range(2):
                for yl in range(2):
                    y = (yh * 2 + yl + (step if c == 0 else -step)) % 4
                    pairs.append(((yh * 2 + c) * 2 + yl, ((y // 2) * 2 + c) * 2 + y % 2))
    else:
        for c in range(2):
            for a in range(4):
                b = (a + (step if c == 0 else -step)) % 4
                pairs.append((c * 4 + a, c * 4 + b))
    return lax.ppermute(value, AXES[axis], pairs)


def add(a, b):
    return (a.astype(F32) + b.astype(F32)).astype(BF)


def sum_of(a, b, c):
    return (a.astype(F32) + b.astype(F32) + c.astype(F32)).astype(BF)


def gates_kernel(gate_ref, up_ref, hid_ref, gu, gut):
    g = gate_ref[...].astype(F32)
    u = up_ref[...].astype(F32)
    h = hid_ref[...].astype(F32)
    sig = 1.0 / (1.0 + jnp.exp(-g))
    gg = h * u * sig * (1.0 + g * (1.0 - sig))
    ug = h * g * sig
    gu[:, :128] = gg.astype(BF)
    gu[:, 128:] = ug.astype(BF)
    gut[:128, :] = gg.T.astype(BF)
    gut[128:, :] = ug.T.astype(BF)


def chunk_kernel(chunks, tab, order, gu, wg, wu, *outs):
    for k, out in zip(chunks, outs):

        @pl.loop(0, 8)
        def _(j):
            base = order[k * 8 + j]
            total = jnp.zeros((TOK, 256), F32)
            for r in range(4):
                sides = []
                for side in range(2):
                    slot = tab[r * 64 + base + side]
                    index = jnp.minimum(slot, SLOTS - 1)
                    block = jnp.concatenate([wg[index], wu[index]], axis=0)
                    sides.append(jnp.where(slot < SLOTS, block, jnp.zeros_like(block)))
                both = jnp.concatenate(sides, axis=1)
                total += jnp.dot(gu[:, r * 256 : (r + 1) * 256], both, preferred_element_type=F32)
            out[j] = total.astype(BF)


PIECE = jax.ShapeDtypeStruct((8, TOK, 256), BF)
VM = pl.BlockSpec(memory_space=pltpu.VMEM)
SM = pl.BlockSpec(memory_space=pltpu.SMEM)
ANY = pl.BlockSpec(memory_space=pl.ANY)


def gates(gate_pre, up_pre, hidden):
    return pl.pallas_call(
        gates_kernel,
        out_shape=[jax.ShapeDtypeStruct((TOK, 1024), BF), jax.ShapeDtypeStruct((1024, TOK), BF)],
        grid=(4,),
        in_specs=[pl.BlockSpec((TOK, 128), lambda r: (0, r))] * 3,
        out_specs=[pl.BlockSpec((TOK, 256), lambda r: (0, r)), pl.BlockSpec((256, TOK), lambda r: (r, 0))],
        compiler_params=pltpu.CompilerParams(vmem_limit_bytes=16 * 1024 * 1024),
        cost_estimate=pl.CostEstimate(flops=1, bytes_accessed=1, transcendentals=0),
        name="gates",
    )(gate_pre, up_pre, hidden)


def terms(chunks, tab, order, gu, wg, wu):
    return pl.pallas_call(
        functools.partial(chunk_kernel, chunks),
        out_shape=[PIECE] * len(chunks),
        in_specs=[SM] * 2 + [VM] * 3,
        out_specs=[VM] * len(chunks),
        compiler_params=pltpu.CompilerParams(vmem_limit_bytes=8 * 1024 * 1024),
        cost_estimate=pl.CostEstimate(flops=1, bytes_accessed=1, transcendentals=0),
        name="terms",
    )(tab, order, gu, wg, wu)


def put(block, grads, slot, sem):
    pltpu.make_async_copy(block, grads.at[slot], sem).start()


def finish(copies, zero, grads, sem):
    @pl.loop(0, copies)
    def _(_):
        pltpu.make_async_copy(zero, grads.at[0], sem).wait()


def same_row_pairs(kind, origin, refs, groups, lrow, lslot, ltile, meta, gts, gate, up, gbuf, ubuf, sem):
    @pl.loop(meta[kind], meta[kind + 1])
    def _(step):
        for pair in range(2):
            pos = step * 4 + pair * 2
            rows = pl.ds(pl.multiple_of(lrow[pos] * 256, 256), 256)
            left = jnp.concatenate([gts[n // 2][g, rows, :] for n, g in enumerate(groups)], axis=1)
            sides = []
            for side in range(2):
                tiles = [ref[ltile[(pos + side) * 4 + n]] for n, ref in enumerate(refs)]
                sides.append(jnp.concatenate(tiles, axis=0))
            total = jnp.dot(left, jnp.concatenate(sides, axis=1), preferred_element_type=F32).astype(BF)
            for side in range(2):
                gbuf[pos + side - origin] = total[:128, side * 128 : side * 128 + 128]
                ubuf[pos + side - origin] = total[128:, side * 128 : side * 128 + 128]
        for n in range(4):
            pos = step * 4 + n

            @pl.when(lslot[pos] < SLOTS)
            def _():
                put(gbuf.at[pos - origin], gate, lslot[pos], sem)
                put(ubuf.at[pos - origin], up, lslot[pos], sem)


def kinds_kernel(kinds, held, lrow, lslot, ltile, meta, gt, gt_c, *rest):
    pieces, (gate, up, gbuf, ubuf, zero, sem) = rest[: len(rest) - 6 - held], rest[-6:]
    origin = meta[kinds[0][0]] * 4
    if not held:
        zero[...] = jnp.zeros((128, 128), BF)

        @pl.loop(meta[8], SLOTS)
        def _(s):
            put(zero, gate, s, sem)
            put(zero, up, s, sem)

        finish(2 * (SLOTS - meta[8]), zero, gate, sem)
    for kind, picks in kinds:
        refs = [pieces[n] for n in picks]
        flip = meta[7]
        groups = (flip, 1 - flip, 1 - flip, flip) if kind == 3 else (0, 1, 0, 1)
        same_row_pairs(kind, origin, refs, groups, lrow, lslot, ltile, meta, (gt, gt_c), gate, up, gbuf, ubuf, sem)
    finish(2 * (meta[9 + kinds[-1][0] + 1] - meta[9 + kinds[0][0]]), zero, gate, sem)


def weight_grads(name, kinds, room, lists, gts, pieces, held=()):
    grads = jax.ShapeDtypeStruct((SLOTS, 128, 128), BF)
    first = 6 + len(pieces)
    return pl.pallas_call(
        functools.partial(kinds_kernel, kinds, len(held)),
        out_shape=[grads] * 2,
        in_specs=[SM] * 4 + [VM] * (2 + len(pieces)) + [ANY] * len(held),
        out_specs=[ANY] * 2,
        scratch_shapes=[
            pltpu.VMEM((room, 128, 128), BF),
            pltpu.VMEM((room, 128, 128), BF),
            pltpu.VMEM((128, 128), BF),
            pltpu.SemaphoreType.DMA,
        ],
        input_output_aliases={first + n: n for n in range(len(held))},
        compiler_params=pltpu.CompilerParams(vmem_limit_bytes=13 * 1024 * 1024),
        cost_estimate=pl.CostEstimate(flops=1, bytes_accessed=1, transcendentals=0),
        name=name,
    )(*lists, *gts, *pieces, *held)


def block_table(block_rows, block_cols, block_count):
    i32 = jnp.int32
    x, z, yl = lax.axis_index("x"), lax.axis_index("z"), lax.axis_index("yl")
    sign = 1 - 2 * lax.axis_index("c")
    slots = jnp.arange(SLOTS, dtype=i32)
    key = jnp.where(slots < block_count[0], block_rows % 4 * 64 + block_cols, -1)
    hit = key[None, :] == jnp.arange(256, dtype=i32)[:, None]
    tab = jnp.min(jnp.where(hit, slots[None, :], SLOTS), axis=1)
    k = jnp.arange(4, dtype=i32)
    xs = (x - sign * k) % 4
    zs = (z - sign * k) % 4
    ys = yl ^ jnp.arange(2, dtype=i32)
    order = (((xs[:, None, None] * 4 + zs[None, :, None]) * 2 + ys[None, None, :]) * 2).reshape(32)
    return tab, order


def slot_lists(block_rows, block_cols, block_count):
    i32 = jnp.int32
    x, z = lax.axis_index("x"), lax.axis_index("z")
    yh, yl = lax.axis_index("yh"), lax.axis_index("yl")
    sign = 1 - 2 * lax.axis_index("c")
    slots = jnp.arange(SLOTS, dtype=i32)
    live = slots < block_count[0]
    row = block_rows % 4
    col = block_cols
    near = (sign * (z - (col >> 2))) % 4
    odd_kind = jnp.where(near == 0, 0, jnp.where(near == 3, 1, jnp.where(near == 1, 2, 5)))
    even_kind = jnp.where(((col >> 1) & 1) == yl, 4, 3)
    kind = jnp.where((col & 1) == 0, even_kind, odd_kind)
    group = kind * 4 + row
    same = (group[:, None] == group[None, :]) & live[None, :]
    rank = jnp.sum(jnp.where(same & (slots[None, :] < slots[:, None]), 1, 0), axis=1)
    groups = jnp.arange(24, dtype=i32)
    count = jnp.sum(jnp.where((group[None, :] == groups[:, None]) & live[None, :], 1, 0), axis=1)
    npair = (count + 1) // 2
    kinds = jnp.arange(6, dtype=i32)
    steps = (jnp.sum(npair.reshape(6, 4), axis=1) + 1) // 2
    edges = jnp.arange(7, dtype=i32)
    before = kinds[None, :] < edges[:, None]
    bounds = jnp.sum(jnp.where(before, steps[None, :], 0), axis=1)
    lives = jnp.sum(jnp.where(before, jnp.sum(count.reshape(6, 4), axis=1)[None, :], 0), axis=1)
    start = jnp.sum(jnp.where(kinds[None, :] < kind[:, None], 2 * steps[None, :], 0), axis=1) + jnp.sum(
        jnp.where((groups[None, :] < group[:, None]) & (groups[None, :] // 4 == kind[:, None]), npair[None, :], 0),
        axis=1,
    )
    place = jnp.where(live, start * 2 + rank, -1)
    at = place[None, :] == jnp.arange(2 * PAIRS, dtype=i32)[:, None]
    lslot = jnp.min(jnp.where(at, slots[None, :], SLOTS), axis=1)
    lrow = jnp.sum(jnp.where(at, row[None, :], 0), axis=1)
    lcol = jnp.sum(jnp.where(at, col[None, :], 0), axis=1)
    cx, cz, cy, par = lcol >> 4, (lcol >> 2) & 3, (lcol >> 1) & 1, lcol & 1
    tiles = []
    for way in (sign, -sign):
        kx = (way * (x - cx)) % 4
        kz = (way * (z - cz)) % 4
        for j in range(2):
            ky = (way * ((yh * 2 + yl) - ((yh ^ j) * 2 + cy))) % 4
            tiles.append(jnp.where(par == 0, kz, ky) * 4 + kx)
    ltile = jnp.stack(tiles, axis=1).reshape(-1)
    flip = jnp.where((yl == 1) == (sign == 1), 0, 1).astype(i32)
    meta = jnp.concatenate([bounds, flip[None], block_count, lives]).astype(i32)
    return lrow, lslot, ltile, meta


def after(value, *others):
    return lax.optimization_barrier((value, *others))[0]


def body(
    activations, gate_pre, up_pre, hidden_grad, gate_blocks, up_blocks, block_rows, block_cols, block_count,
):
    tab, order = block_table(block_rows, block_cols, block_count)
    blocks = (gate_blocks, up_blocks)
    gu, gut = gates(gate_pre, up_pre, hidden_grad)
    other = shift(gut, "yh", 1)
    both = after(jnp.stack([activations[:, :128], activations[:, 128:]]), gut)
    near = [both] + [shift(both, "x", k) for k in (1, 2, 3)]
    (t2,) = terms((2,), tab, order, gu, *blocks)
    ahead = shift(t2, "x", 1)
    even = after(jnp.stack([v[0] for v in near]), t2)
    odd = after(jnp.stack([v[1] for v in near]), t2, other)
    evens, odds = [even], [odd]
    evens.append(shift(even, "z", 1))
    odds.append(shift(odd, "y", 1))
    (t1,) = terms((1,), tab, order, after(gu, even, odd), *blocks)
    back = shift(t1, "x", -1)
    evens.append(shift(after(evens[1], t1), "z", 1))
    odds.append(shift(after(odds[1], t1), "y", 1))
    t3, t0 = terms((3, 0), tab, order, after(gu, evens[1], odds[1]), *blocks)
    evens.append(shift(after(evens[2], t3), "z", 1))
    odds.append(shift(after(odds[2], t3), "y", 1))
    moving = add(after(ahead, evens[2], odds[2]), t3)
    even_0 = after(jnp.concatenate(evens), t0, moving)
    odd_0 = after(jnp.concatenate(odds), t0, moving)
    even_1, even_3 = shift(even_0, "y", 1), shift(even_0, "y", -1)
    odd_1, odd_3 = shift(odd_0, "z", 1), shift(odd_0, "z", -1)
    ahead = shift(moving, "x", 1)
    rows_late, cols_late, count_late = (after(v, even_0, odd_0) for v in (block_rows, block_cols, block_count))
    lrow, lslot, ltile, meta = slot_lists(rows_late, cols_late, count_late)
    mine = sum_of(t0, ahead, back).reshape(4, 2, TOK, 256)
    own = after(jnp.stack([gut, other]), mine)
    own_c = shift(own, "c", 1)
    odd_0c = shift(after(odd_0, mine), "c", 1)

    def grads_of(name, kinds, room, pieces, held=(), wait=()):
        return weight_grads(name, kinds, room, (lrow, lslot, ltile, after(meta, *wait)), (own, own_c), pieces, held)

    even_2 = shift(after(even_1, even_3), "y", 1)
    odd_2 = shift(after(odd_1, odd_3), "z", 1)
    odd_1c, odd_3c = shift(odd_1, "c", 1), shift(odd_3, "c", 1)
    even_1c, even_3c = (shift(after(v, odd_1c, odd_3c, odd_0c), "c", 1) for v in (even_1, even_3))
    grads = grads_of("grads_0", ((0, (0, 0, 1, 1)),), 40, (odd_0, odd_0c))
    grads = grads_of("grads_1", ((1, (0, 0, 1, 1)),), 40, (odd_3, odd_1c), grads)
    grads = grads_of("grads_2", ((2, (0, 0, 1, 1)),), 40, (odd_1, odd_3c), grads)
    even_0c = shift(after(even_0, grads[0]), "c", 1)
    even_2 = after(even_2, grads[0])
    ahead = shift(after(mine[2], odd_3c), "z", 1)
    back = shift(after(mine[1], odd_3c), "z", -1)
    grads = grads_of("grads_3", ((3, (0, 1, 2, 3)),), 72, (even_1, even_3, even_1c, even_3c), grads, (even_2,))
    even_2c = shift(even_2, "c", 1)
    odd_2c = shift(odd_2, "c", 1)
    ahead = add(after(ahead, grads[0], back), mine[3])
    grads = grads_of(
        "grads_4", ((4, (0, 1, 2, 3)),), 72, (even_0, even_2, even_0c, even_2c), grads, (ahead, odd_2)
    )
    ahead = after(shift(ahead, "z", 1), grads[0])
    send = sum_of(mine[0, 1], ahead[1], back[1])
    keep = mine[0, 0].astype(F32) + ahead[0].astype(F32) + back[0].astype(F32)
    gate_grad, up_grad = grads_of("grads_5", ((5, (0, 0, 1, 1)),), 40, (odd_2, odd_2c), grads, (send,))
    input_grad = (keep + after(shift(send, "yl", 1), gate_grad).astype(F32)).astype(BF)
    return input_grad, gate_grad, up_grad


def solution(mesh):
    fine = Mesh(mesh.devices.reshape(2, 2, 4, 4, 2), ("yh", "c", "x", "z", "yl"))
    tok, wt = ("yh", "c"), ("x", "z", "yl")
    in_specs = (P(tok, wt),) * 4 + (P(wt, None, None),) * 2 + (P(wt),) * 3
    out_specs = (P(tok, wt), P(wt, None, None), P(wt, None, None))
    return jax.shard_map(body, mesh=fine, in_specs=in_specs, out_specs=out_specs, check_vma=False)
```

```python
import functools

import jax
import jax.numpy as jnp
from jax import lax
from jax.experimental import pallas as pl
from jax.experimental.pallas import tpu as pltpu
from jax.sharding import Mesh
from jax.sharding import PartitionSpec as P

BF = jnp.bfloat16
F32 = jnp.float32
AXES = {"x": ("c", "x"), "z": ("c", "z"), "y": ("yh", "c", "yl")}
SIZES = {"yh": 2, "c": 2, "x": 4, "z": 4, "yl": 2}
TOK = 384
SLOTS = 128
PAIRS = 82


def shift(value, axis, step):
    pairs = []
    if axis in ("yh", "c", "yl"):
        return lax.ppermute(value, axis, [(0, 1), (1, 0)])
    if axis == "y":
        for yh in range(2):
            for c in range(2):
                for yl in range(2):
                    y = (yh * 2 + yl + (step if c == 0 else -step)) % 4
                    pairs.append(((yh * 2 + c) * 2 + yl, ((y // 2) * 2 + c) * 2 + y % 2))
    else:
        for c in range(2):
            for a in range(4):
                b = (a + (step if c == 0 else -step)) % 4
                pairs.append((c * 4 + a, c * 4 + b))
    return lax.ppermute(value, AXES[axis], pairs)


def add(a, b):
    return (a.astype(F32) + b.astype(F32)).astype(BF)


def sum_of(a, b, c):
    return (a.astype(F32) + b.astype(F32) + c.astype(F32)).astype(BF)


def gates_kernel(gate_ref, up_ref, hid_ref, gu, gut):
    g = gate_ref[...].astype(F32)
    u = up_ref[...].astype(F32)
    h = hid_ref[...].astype(F32)
    sig = 1.0 / (1.0 + jnp.exp(-g))
    gg = h * u * sig * (1.0 + g * (1.0 - sig))
    ug = h * g * sig
    gu[:, :128] = gg.astype(BF)
    gu[:, 128:] = ug.astype(BF)
    gut[:128, :] = gg.T.astype(BF)
    gut[128:, :] = ug.T.astype(BF)


def chunk_kernel(chunks, tab, order, gu, wg, wu, *outs):
    for k, out in zip(chunks, outs):

        @pl.loop(0, 8)
        def _(j):
            base = order[k * 8 + j]
            total = jnp.zeros((TOK, 256), F32)
            for r in range(4):
                sides = []
                for side in range(2):
                    slot = tab[r * 64 + base + side]
                    index = jnp.minimum(slot, SLOTS - 1)
                    block = jnp.concatenate([wg[index], wu[index]], axis=0)
                    sides.append(jnp.where(slot < SLOTS, block, jnp.zeros_like(block)))
                both = jnp.concatenate(sides, axis=1)
                total += jnp.dot(gu[:, r * 256 : (r + 1) * 256], both, preferred_element_type=F32)
            out[j] = total.astype(BF)


PIECE = jax.ShapeDtypeStruct((8, TOK, 256), BF)
VM = pl.BlockSpec(memory_space=pltpu.VMEM)
SM = pl.BlockSpec(memory_space=pltpu.SMEM)
ANY = pl.BlockSpec(memory_space=pl.ANY)


def gates(gate_pre, up_pre, hidden):
    return pl.pallas_call(
        gates_kernel,
        out_shape=[jax.ShapeDtypeStruct((TOK, 1024), BF), jax.ShapeDtypeStruct((1024, TOK), BF)],
        grid=(4,),
        in_specs=[pl.BlockSpec((TOK, 128), lambda r: (0, r))] * 3,
        out_specs=[pl.BlockSpec((TOK, 256), lambda r: (0, r)), pl.BlockSpec((256, TOK), lambda r: (r, 0))],
        compiler_params=pltpu.CompilerParams(vmem_limit_bytes=16 * 1024 * 1024),
        cost_estimate=pl.CostEstimate(flops=1, bytes_accessed=1, transcendentals=0),
        name="gates",
    )(gate_pre, up_pre, hidden)


def terms(chunks, tab, order, gu, wg, wu):
    return pl.pallas_call(
        functools.partial(chunk_kernel, chunks),
        out_shape=[PIECE] * len(chunks),
        in_specs=[SM] * 2 + [VM] * 3,
        out_specs=[VM] * len(chunks),
        compiler_params=pltpu.CompilerParams(vmem_limit_bytes=8 * 1024 * 1024),
        cost_estimate=pl.CostEstimate(flops=1, bytes_accessed=1, transcendentals=0),
        name="terms",
    )(tab, order, gu, wg, wu)


def put(block, grads, slot, sem):
    pltpu.make_async_copy(block, grads.at[slot], sem).start()


def finish(copies, zero, grads, sem):
    @pl.loop(0, copies)
    def _(_):
        pltpu.make_async_copy(zero, grads.at[0], sem).wait()


def same_row_pairs(kind, origin, refs, groups, lrow, lslot, ltile, meta, gts, gate, up, gbuf, ubuf, sem):
    @pl.loop(meta[kind], meta[kind + 1])
    def _(step):
        for pair in range(2):
            pos = step * 4 + pair * 2
            rows = pl.ds(pl.multiple_of(lrow[pos] * 256, 256), 256)
            left = jnp.concatenate([gts[n // 2][g, rows, :] for n, g in enumerate(groups)], axis=1)
            sides = []
            for side in range(2):
                tiles = [ref[ltile[(pos + side) * 4 + n]] for n, ref in enumerate(refs)]
                sides.append(jnp.concatenate(tiles, axis=0))
            total = jnp.dot(left, jnp.concatenate(sides, axis=1), preferred_element_type=F32).astype(BF)
            for side in range(2):
                gbuf[pos + side - origin] = total[:128, side * 128 : side * 128 + 128]
                ubuf[pos + side - origin] = total[128:, side * 128 : side * 128 + 128]
        for n in range(4):
            pos = step * 4 + n

            @pl.when(lslot[pos] < SLOTS)
            def _():
                put(gbuf.at[pos - origin], gate, lslot[pos], sem)
                put(ubuf.at[pos - origin], up, lslot[pos], sem)


def kinds_kernel(kinds, held, lrow, lslot, ltile, meta, gt, gt_c, *rest):
    pieces, (gate, up, gbuf, ubuf, zero, sem) = rest[: len(rest) - 6 - held], rest[-6:]
    origin = meta[kinds[0][0]] * 4
    if not held:
        zero[...] = jnp.zeros((128, 128), BF)

        @pl.loop(meta[8], SLOTS)
        def _(s):
            put(zero, gate, s, sem)
            put(zero, up, s, sem)

        finish(2 * (SLOTS - meta[8]), zero, gate, sem)
    for kind, picks in kinds:
        refs = [pieces[n] for n in picks]
        flip = meta[7]
        groups = (flip, 1 - flip, 1 - flip, flip) if kind == 3 else (0, 1, 0, 1)
        same_row_pairs(kind, origin, refs, groups, lrow, lslot, ltile, meta, (gt, gt_c), gate, up, gbuf, ubuf, sem)
    finish(2 * (meta[9 + kinds[-1][0] + 1] - meta[9 + kinds[0][0]]), zero, gate, sem)


def weight_grads(name, kinds, room, lists, gts, pieces, held=()):
    grads = jax.ShapeDtypeStruct((SLOTS, 128, 128), BF)
    first = 6 + len(pieces)
    return pl.pallas_call(
        functools.partial(kinds_kernel, kinds, len(held)),
        out_shape=[grads] * 2,
        in_specs=[SM] * 4 + [VM] * (2 + len(pieces)) + [ANY] * len(held),
        out_specs=[ANY] * 2,
        scratch_shapes=[
            pltpu.VMEM((room, 128, 128), BF),
            pltpu.VMEM((room, 128, 128), BF),
            pltpu.VMEM((128, 128), BF),
            pltpu.SemaphoreType.DMA,
        ],
        input_output_aliases={first + n: n for n in range(len(held))},
        compiler_params=pltpu.CompilerParams(vmem_limit_bytes=13 * 1024 * 1024),
        cost_estimate=pl.CostEstimate(flops=1, bytes_accessed=1, transcendentals=0),
        name=name,
    )(*lists, *gts, *pieces, *held)


def block_table(block_rows, block_cols, block_count):
    i32 = jnp.int32
    x, z, yl = lax.axis_index("x"), lax.axis_index("z"), lax.axis_index("yl")
    sign = 1 - 2 * lax.axis_index("c")
    slots = jnp.arange(SLOTS, dtype=i32)
    key = jnp.where(slots < block_count[0], block_rows % 4 * 64 + block_cols, -1)
    hit = key[None, :] == jnp.arange(256, dtype=i32)[:, None]
    tab = jnp.min(jnp.where(hit, slots[None, :], SLOTS), axis=1)
    k = jnp.arange(4, dtype=i32)
    xs = (x - sign * k) % 4
    zs = (z - sign * k) % 4
    ys = yl ^ jnp.arange(2, dtype=i32)
    order = (((xs[:, None, None] * 4 + zs[None, :, None]) * 2 + ys[None, None, :]) * 2).reshape(32)
    return tab, order


def slot_lists(block_rows, block_cols, block_count):
    i32 = jnp.int32
    x, z = lax.axis_index("x"), lax.axis_index("z")
    yh, yl = lax.axis_index("yh"), lax.axis_index("yl")
    sign = 1 - 2 * lax.axis_index("c")
    slots = jnp.arange(SLOTS, dtype=i32)
    live = slots < block_count[0]
    row = block_rows % 4
    col = block_cols
    near = (sign * (z - (col >> 2))) % 4
    odd_kind = jnp.where(near == 0, 0, jnp.where(near == 3, 1, jnp.where(near == 1, 2, 5)))
    even_kind = jnp.where(((col >> 1) & 1) == yl, 4, 3)
    kind = jnp.where((col & 1) == 0, even_kind, odd_kind)
    group = kind * 4 + row
    same = (group[:, None] == group[None, :]) & live[None, :]
    rank = jnp.sum(jnp.where(same & (slots[None, :] < slots[:, None]), 1, 0), axis=1)
    groups = jnp.arange(24, dtype=i32)
    count = jnp.sum(jnp.where((group[None, :] == groups[:, None]) & live[None, :], 1, 0), axis=1)
    npair = (count + 1) // 2
    kinds = jnp.arange(6, dtype=i32)
    steps = (jnp.sum(npair.reshape(6, 4), axis=1) + 1) // 2
    edges = jnp.arange(7, dtype=i32)
    before = kinds[None, :] < edges[:, None]
    bounds = jnp.sum(jnp.where(before, steps[None, :], 0), axis=1)
    lives = jnp.sum(jnp.where(before, jnp.sum(count.reshape(6, 4), axis=1)[None, :], 0), axis=1)
    start = jnp.sum(jnp.where(kinds[None, :] < kind[:, None], 2 * steps[None, :], 0), axis=1) + jnp.sum(
        jnp.where((groups[None, :] < group[:, None]) & (groups[None, :] // 4 == kind[:, None]), npair[None, :], 0),
        axis=1,
    )
    place = jnp.where(live, start * 2 + rank, -1)
    at = place[None, :] == jnp.arange(2 * PAIRS, dtype=i32)[:, None]
    lslot = jnp.min(jnp.where(at, slots[None, :], SLOTS), axis=1)
    lrow = jnp.sum(jnp.where(at, row[None, :], 0), axis=1)
    lcol = jnp.sum(jnp.where(at, col[None, :], 0), axis=1)
    cx, cz, cy, par = lcol >> 4, (lcol >> 2) & 3, (lcol >> 1) & 1, lcol & 1
    tiles = []
    for way in (sign, -sign):
        kx = (way * (x - cx)) % 4
        kz = (way * (z - cz)) % 4
        for j in range(2):
            ky = (way * ((yh * 2 + yl) - ((yh ^ j) * 2 + cy))) % 4
            tiles.append(jnp.where(par == 0, kz, ky) * 4 + kx)
    ltile = jnp.stack(tiles, axis=1).reshape(-1)
    flip = jnp.where((yl == 1) == (sign == 1), 0, 1).astype(i32)
    meta = jnp.concatenate([bounds, flip[None], block_count, lives]).astype(i32)
    return lrow, lslot, ltile, meta


def after(value, *others):
    return lax.optimization_barrier((value, *others))[0]


def body(
    activations, gate_pre, up_pre, hidden_grad, gate_blocks, up_blocks, block_rows, block_cols, block_count,
):
    tab, order = block_table(block_rows, block_cols, block_count)
    blocks = (gate_blocks, up_blocks)
    gu, gut = gates(gate_pre, up_pre, hidden_grad)
    other = shift(gut, "yh", 1)
    both = after(jnp.stack([activations[:, :128], activations[:, 128:]]), gut)
    near = [both] + [shift(both, "x", k) for k in (1, 2, 3)]
    (t2,) = terms((2,), tab, order, gu, *blocks)
    ahead = shift(t2, "x", 1)
    even = after(jnp.stack([v[0] for v in near]), t2)
    odd = after(jnp.stack([v[1] for v in near]), t2, other)
    evens, odds = [even], [odd]
    evens.append(shift(even, "z", 1))
    odds.append(shift(odd, "y", 1))
    (t1,) = terms((1,), tab, order, after(gu, even, odd), *blocks)
    back = shift(t1, "x", -1)
    evens.append(shift(after(evens[1], t1), "z", 1))
    odds.append(shift(after(odds[1], t1), "y", 1))
    t3, t0 = terms((3, 0), tab, order, after(gu, evens[1], odds[1]), *blocks)
    evens.append(shift(after(evens[2], t3), "z", 1))
    odds.append(shift(after(odds[2], t3), "y", 1))
    moving = add(after(ahead, evens[2], odds[2]), t3)
    even_0, odd_0 = lax.optimization_barrier((jnp.concatenate(evens), jnp.concatenate(odds), t0, moving))[:2]
    even_1, even_3 = shift(even_0, "y", 1), shift(even_0, "y", -1)
    odd_1, odd_3 = shift(odd_0, "z", 1), shift(odd_0, "z", -1)
    ahead = shift(moving, "x", 1)
    rows_late, cols_late, count_late = (after(v, even_0, odd_0) for v in (block_rows, block_cols, block_count))
    lrow, lslot, ltile, meta = slot_lists(rows_late, cols_late, count_late)
    mine = sum_of(t0, ahead, back).reshape(4, 2, TOK, 256)
    own = after(jnp.stack([gut, other]), mine)
    own_c = shift(own, "c", 1)
    odd_0c = shift(after(odd_0, mine), "c", 1)

    def grads_of(name, kinds, room, pieces, held=(), wait=()):
        return weight_grads(name, kinds, room, (lrow, lslot, ltile, after(meta, *wait)), (own, own_c), pieces, held)

    even_2 = shift(after(even_1, even_3), "y", 1)
    odd_2 = shift(after(odd_1, odd_3), "z", 1)
    odd_1c, odd_3c = shift(odd_1, "c", 1), shift(odd_3, "c", 1)
    even_1c, even_3c = (shift(after(v, odd_1c, odd_3c, odd_0c), "c", 1) for v in (even_1, even_3))
    grads = grads_of("grads_0", ((0, (0, 0, 1, 1)),), 40, (odd_0, odd_0c))
    grads = grads_of("grads_1", ((1, (0, 0, 1, 1)),), 40, (odd_3, odd_1c), grads)
    grads = grads_of("grads_2", ((2, (0, 0, 1, 1)),), 40, (odd_1, odd_3c), grads)
    even_0c = shift(after(even_0, grads[0]), "c", 1)
    even_2 = after(even_2, grads[0])
    ahead = shift(after(mine[2], odd_3c), "z", 1)
    back = shift(after(mine[1], odd_3c), "z", -1)
    grads = grads_of("grads_3", ((3, (0, 1, 2, 3)),), 72, (even_1, even_3, even_1c, even_3c), grads, (even_2,))
    even_2c = shift(even_2, "c", 1)
    odd_2c = shift(odd_2, "c", 1)
    ahead = add(after(ahead, grads[0], back), mine[3])
    grads = grads_of(
        "grads_4", ((4, (0, 1, 2, 3)),), 72, (even_0, even_2, even_0c, even_2c), grads, (ahead, odd_2)
    )
    ahead = after(shift(ahead, "z", 1), grads[0])
    send = sum_of(mine[0, 1], ahead[1], back[1])
    keep = mine[0, 0].astype(F32) + ahead[0].astype(F32) + back[0].astype(F32)
    gate_grad, up_grad = grads_of("grads_5", ((5, (0, 0, 1, 1)),), 40, (odd_2, odd_2c), grads, (send,))
    input_grad = (keep + after(shift(send, "yl", 1), gate_grad).astype(F32)).astype(BF)
    return input_grad, gate_grad, up_grad


def solution(mesh):
    fine = Mesh(mesh.devices.reshape(2, 2, 4, 4, 2), ("yh", "c", "x", "z", "yl"))
    tok, wt = ("yh", "c"), ("x", "z", "yl")
    in_specs = (P(tok, wt),) * 4 + (P(wt, None, None),) * 2 + (P(wt),) * 3
    out_specs = (P(tok, wt), P(wt, None, None), P(wt, None, None))
    return jax.shard_map(body, mesh=fine, in_specs=in_specs, out_specs=out_specs, check_vma=False)
```

```python
import functools

import jax
import jax.numpy as jnp
from jax import lax
from jax.experimental import pallas as pl
from jax.experimental.pallas import tpu as pltpu
from jax.sharding import Mesh
from jax.sharding import PartitionSpec as P

BF = jnp.bfloat16
F32 = jnp.float32
AXES = {"x": ("c", "x"), "z": ("c", "z"), "y": ("yh", "c", "yl")}
SIZES = {"yh": 2, "c": 2, "x": 4, "z": 4, "yl": 2}
TOK = 384
SLOTS = 128
PAIRS = 82


def shift(value, axis, step):
    pairs = []
    if axis in ("yh", "c", "yl"):
        return lax.ppermute(value, axis, [(0, 1), (1, 0)])
    if axis == "y":
        for yh in range(2):
            for c in range(2):
                for yl in range(2):
                    y = (yh * 2 + yl + (step if c == 0 else -step)) % 4
                    pairs.append(((yh * 2 + c) * 2 + yl, ((y // 2) * 2 + c) * 2 + y % 2))
    else:
        for c in range(2):
            for a in range(4):
                b = (a + (step if c == 0 else -step)) % 4
                pairs.append((c * 4 + a, c * 4 + b))
    return lax.ppermute(value, AXES[axis], pairs)


def add(a, b):
    return (a.astype(F32) + b.astype(F32)).astype(BF)


def sum_of(a, b, c):
    return (a.astype(F32) + b.astype(F32) + c.astype(F32)).astype(BF)


def gates_kernel(gate_ref, up_ref, hid_ref, gu, gut):
    g = gate_ref[...].astype(F32)
    u = up_ref[...].astype(F32)
    h = hid_ref[...].astype(F32)
    sig = 1.0 / (1.0 + jnp.exp(-g))
    gg = h * u * sig * (1.0 + g * (1.0 - sig))
    ug = h * g * sig
    gu[:, :128] = gg.astype(BF)
    gu[:, 128:] = ug.astype(BF)
    gut[:128, :] = gg.T.astype(BF)
    gut[128:, :] = ug.T.astype(BF)


def chunk_kernel(chunks, tab, order, gu, wg, wu, *outs):
    for k, out in zip(chunks, outs):

        @pl.loop(0, 8)
        def _(j):
            base = order[k * 8 + j]
            total = jnp.zeros((TOK, 256), F32)
            for r in range(4):
                sides = []
                for side in range(2):
                    slot = tab[r * 64 + base + side]
                    index = jnp.minimum(slot, SLOTS - 1)
                    block = jnp.concatenate([wg[index], wu[index]], axis=0)
                    sides.append(jnp.where(slot < SLOTS, block, jnp.zeros_like(block)))
                both = jnp.concatenate(sides, axis=1)
                total += jnp.dot(gu[:, r * 256 : (r + 1) * 256], both, preferred_element_type=F32)
            out[j] = total.astype(BF)


PIECE = jax.ShapeDtypeStruct((8, TOK, 256), BF)
VM = pl.BlockSpec(memory_space=pltpu.VMEM)
SM = pl.BlockSpec(memory_space=pltpu.SMEM)
ANY = pl.BlockSpec(memory_space=pl.ANY)


def gates(gate_pre, up_pre, hidden):
    return pl.pallas_call(
        gates_kernel,
        out_shape=[jax.ShapeDtypeStruct((TOK, 1024), BF), jax.ShapeDtypeStruct((1024, TOK), BF)],
        grid=(4,),
        in_specs=[pl.BlockSpec((TOK, 128), lambda r: (0, r))] * 3,
        out_specs=[pl.BlockSpec((TOK, 256), lambda r: (0, r)), pl.BlockSpec((256, TOK), lambda r: (r, 0))],
        compiler_params=pltpu.CompilerParams(vmem_limit_bytes=16 * 1024 * 1024),
        cost_estimate=pl.CostEstimate(flops=1, bytes_accessed=1, transcendentals=0),
        name="gates",
    )(gate_pre, up_pre, hidden)


def terms(chunks, tab, order, gu, wg, wu):
    return pl.pallas_call(
        functools.partial(chunk_kernel, chunks),
        out_shape=[PIECE] * len(chunks),
        in_specs=[SM] * 2 + [VM] * 3,
        out_specs=[VM] * len(chunks),
        compiler_params=pltpu.CompilerParams(vmem_limit_bytes=8 * 1024 * 1024),
        cost_estimate=pl.CostEstimate(flops=1, bytes_accessed=1, transcendentals=0),
        name="terms",
    )(tab, order, gu, wg, wu)


def put(block, grads, slot, sem):
    pltpu.make_async_copy(block, grads.at[slot], sem).start()


def finish(copies, zero, grads, sem):
    @pl.loop(0, copies)
    def _(_):
        pltpu.make_async_copy(zero, grads.at[0], sem).wait()


def same_row_pairs(kind, origin, refs, groups, lrow, lslot, ltile, meta, gts, gate, up, gbuf, ubuf, sem):
    @pl.loop(meta[kind], meta[kind + 1])
    def _(step):
        for pair in range(2):
            pos = step * 4 + pair * 2
            rows = pl.ds(pl.multiple_of(lrow[pos] * 256, 256), 256)
            left = jnp.concatenate([gts[n // 2][g, rows, :] for n, g in enumerate(groups)], axis=1)
            sides = []
            for side in range(2):
                tiles = [ref[ltile[(pos + side) * 4 + n]] for n, ref in enumerate(refs)]
                sides.append(jnp.concatenate(tiles, axis=0))
            total = jnp.dot(left, jnp.concatenate(sides, axis=1), preferred_element_type=F32).astype(BF)
            for side in range(2):
                gbuf[pos + side - origin] = total[:128, side * 128 : side * 128 + 128]
                ubuf[pos + side - origin] = total[128:, side * 128 : side * 128 + 128]
        for n in range(4):
            pos = step * 4 + n

            @pl.when(lslot[pos] < SLOTS)
            def _():
                put(gbuf.at[pos - origin], gate, lslot[pos], sem)
                put(ubuf.at[pos - origin], up, lslot[pos], sem)


def kinds_kernel(kinds, held, lrow, lslot, ltile, meta, gt, gt_c, *rest):
    pieces, (gate, up, gbuf, ubuf, zero, sem) = rest[: len(rest) - 6 - held], rest[-6:]
    origin = meta[kinds[0][0]] * 4
    if not held:
        zero[...] = jnp.zeros((128, 128), BF)

        @pl.loop(meta[8], SLOTS)
        def _(s):
            put(zero, gate, s, sem)
            put(zero, up, s, sem)

        finish(2 * (SLOTS - meta[8]), zero, gate, sem)
    for kind, picks in kinds:
        refs = [pieces[n] for n in picks]
        flip = meta[7]
        groups = (flip, 1 - flip, 1 - flip, flip) if kind == 3 else (0, 1, 0, 1)
        same_row_pairs(kind, origin, refs, groups, lrow, lslot, ltile, meta, (gt, gt_c), gate, up, gbuf, ubuf, sem)
    finish(2 * (meta[9 + kinds[-1][0] + 1] - meta[9 + kinds[0][0]]), zero, gate, sem)


def weight_grads(name, kinds, room, lists, gts, pieces, held=()):
    grads = jax.ShapeDtypeStruct((SLOTS, 128, 128), BF)
    first = 6 + len(pieces)
    return pl.pallas_call(
        functools.partial(kinds_kernel, kinds, len(held)),
        out_shape=[grads] * 2,
        in_specs=[SM] * 4 + [VM] * (2 + len(pieces)) + [ANY] * len(held),
        out_specs=[ANY] * 2,
        scratch_shapes=[
            pltpu.VMEM((room, 128, 128), BF),
            pltpu.VMEM((room, 128, 128), BF),
            pltpu.VMEM((128, 128), BF),
            pltpu.SemaphoreType.DMA,
        ],
        input_output_aliases={first + n: n for n in range(len(held))},
        compiler_params=pltpu.CompilerParams(vmem_limit_bytes=13 * 1024 * 1024),
        cost_estimate=pl.CostEstimate(flops=1, bytes_accessed=1, transcendentals=0),
        name=name,
    )(*lists, *gts, *pieces, *held)


def block_table(block_rows, block_cols, block_count):
    i32 = jnp.int32
    x, z, yl = lax.axis_index("x"), lax.axis_index("z"), lax.axis_index("yl")
    sign = 1 - 2 * lax.axis_index("c")
    slots = jnp.arange(SLOTS, dtype=i32)
    key = jnp.where(slots < block_count[0], block_rows % 4 * 64 + block_cols, -1)
    hit = key[None, :] == jnp.arange(256, dtype=i32)[:, None]
    tab = jnp.min(jnp.where(hit, slots[None, :], SLOTS), axis=1)
    k = jnp.arange(4, dtype=i32)
    xs = (x - sign * k) % 4
    zs = (z - sign * k) % 4
    ys = yl ^ jnp.arange(2, dtype=i32)
    order = (((xs[:, None, None] * 4 + zs[None, :, None]) * 2 + ys[None, None, :]) * 2).reshape(32)
    return tab, order


def slot_lists(block_rows, block_cols, block_count):
    i32 = jnp.int32
    x, z = lax.axis_index("x"), lax.axis_index("z")
    yh, yl = lax.axis_index("yh"), lax.axis_index("yl")
    sign = 1 - 2 * lax.axis_index("c")
    slots = jnp.arange(SLOTS, dtype=i32)
    live = slots < block_count[0]
    row = block_rows % 4
    col = block_cols
    near = (sign * (z - (col >> 2))) % 4
    odd_kind = jnp.where(near == 0, 0, jnp.where(near == 3, 1, jnp.where(near == 1, 2, 5)))
    even_kind = jnp.where(((col >> 1) & 1) == yl, 4, 3)
    kind = jnp.where((col & 1) == 0, even_kind, odd_kind)
    group = kind * 4 + row
    same = (group[:, None] == group[None, :]) & live[None, :]
    rank = jnp.sum(jnp.where(same & (slots[None, :] < slots[:, None]), 1, 0), axis=1)
    groups = jnp.arange(24, dtype=i32)
    count = jnp.sum(jnp.where((group[None, :] == groups[:, None]) & live[None, :], 1, 0), axis=1)
    npair = (count + 1) // 2
    kinds = jnp.arange(6, dtype=i32)
    steps = (jnp.sum(npair.reshape(6, 4), axis=1) + 1) // 2
    edges = jnp.arange(7, dtype=i32)
    before = kinds[None, :] < edges[:, None]
    bounds = jnp.sum(jnp.where(before, steps[None, :], 0), axis=1)
    lives = jnp.sum(jnp.where(before, jnp.sum(count.reshape(6, 4), axis=1)[None, :], 0), axis=1)
    start = jnp.sum(jnp.where(kinds[None, :] < kind[:, None], 2 * steps[None, :], 0), axis=1) + jnp.sum(
        jnp.where((groups[None, :] < group[:, None]) & (groups[None, :] // 4 == kind[:, None]), npair[None, :], 0),
        axis=1,
    )
    place = jnp.where(live, start * 2 + rank, -1)
    at = place[None, :] == jnp.arange(2 * PAIRS, dtype=i32)[:, None]
    lslot = jnp.min(jnp.where(at, slots[None, :], SLOTS), axis=1)
    lrow = jnp.sum(jnp.where(at, row[None, :], 0), axis=1)
    lcol = jnp.sum(jnp.where(at, col[None, :], 0), axis=1)
    cx, cz, cy, par = lcol >> 4, (lcol >> 2) & 3, (lcol >> 1) & 1, lcol & 1
    tiles = []
    for way in (sign, -sign):
        kx = (way * (x - cx)) % 4
        kz = (way * (z - cz)) % 4
        for j in range(2):
            ky = (way * ((yh * 2 + yl) - ((yh ^ j) * 2 + cy))) % 4
            tiles.append(jnp.where(par == 0, kz, ky) * 4 + kx)
    ltile = jnp.stack(tiles, axis=1).reshape(-1)
    flip = jnp.where((yl == 1) == (sign == 1), 0, 1).astype(i32)
    meta = jnp.concatenate([bounds, flip[None], block_count, lives]).astype(i32)
    return lrow, lslot, ltile, meta


def after(value, *others):
    return lax.optimization_barrier((value, *others))[0]


def body(
    activations, gate_pre, up_pre, hidden_grad, gate_blocks, up_blocks, block_rows, block_cols, block_count,
):
    tab, order = block_table(block_rows, block_cols, block_count)
    blocks = (gate_blocks, up_blocks)
    gu, gut = gates(gate_pre, up_pre, hidden_grad)
    other = shift(gut, "yh", 1)
    both = after(jnp.stack([activations[:, :128], activations[:, 128:]]), gut)
    near = [both] + [shift(both, "x", k) for k in (1, 2, 3)]
    (t2,) = terms((2,), tab, order, gu, *blocks)
    ahead = shift(t2, "x", 1)
    even = after(jnp.stack([v[0] for v in near]), t2)
    odd = after(jnp.stack([v[1] for v in near]), t2, other)
    evens, odds = [even], [odd]
    evens.append(shift(even, "z", 1))
    odds.append(shift(odd, "y", 1))
    (t1,) = terms((1,), tab, order, after(gu, even, odd), *blocks)
    back = shift(t1, "x", -1)
    evens.append(shift(after(evens[1], t1), "z", 1))
    odds.append(shift(after(odds[1], t1), "y", 1))
    t3, t0 = terms((3, 0), tab, order, after(gu, evens[1], odds[1]), *blocks)
    evens.append(shift(after(evens[2], t3), "z", 1))
    odds.append(shift(after(odds[2], t3), "y", 1))
    moving = add(after(ahead, evens[3], odds[3]), t3)
    even_0, odd_0 = lax.optimization_barrier((jnp.concatenate(evens), jnp.concatenate(odds), t0, moving))[:2]
    even_1, even_3 = shift(even_0, "y", 1), shift(even_0, "y", -1)
    odd_1, odd_3 = shift(odd_0, "z", 1), shift(odd_0, "z", -1)
    ahead = shift(moving, "x", 1)
    rows_late, cols_late, count_late = (after(v, even_0, odd_0) for v in (block_rows, block_cols, block_count))
    lrow, lslot, ltile, meta = slot_lists(rows_late, cols_late, count_late)
    mine = sum_of(t0, ahead, back).reshape(4, 2, TOK, 256)
    own = after(jnp.stack([gut, other]), mine)
    own_c = shift(own, "c", 1)
    odd_0c = shift(after(odd_0, mine), "c", 1)

    def grads_of(name, kinds, room, pieces, held=(), wait=()):
        return weight_grads(name, kinds, room, (lrow, lslot, ltile, after(meta, *wait)), (own, own_c), pieces, held)

    even_2 = shift(after(even_1, even_3), "y", 1)
    odd_2 = shift(after(odd_1, odd_3), "z", 1)
    odd_1c, odd_3c = shift(odd_1, "c", 1), shift(odd_3, "c", 1)
    even_1c, even_3c = (shift(after(v, odd_1c, odd_3c, odd_0c), "c", 1) for v in (even_1, even_3))
    grads = grads_of("grads_0", ((0, (0, 0, 1, 1)),), 40, (odd_0, odd_0c))
    grads = grads_of("grads_1", ((1, (0, 0, 1, 1)),), 40, (odd_3, odd_1c), grads)
    grads = grads_of("grads_2", ((2, (0, 0, 1, 1)),), 40, (odd_1, odd_3c), grads)
    even_0c = shift(after(even_0, grads[0]), "c", 1)
    even_2 = after(even_2, grads[0])
    ahead = shift(after(mine[2], odd_3c), "z", 1)
    back = shift(after(mine[1], odd_3c), "z", -1)
    grads = grads_of("grads_3", ((3, (0, 1, 2, 3)),), 72, (even_1, even_3, even_1c, even_3c), grads, (even_2,))
    even_2c = shift(even_2, "c", 1)
    odd_2c = shift(odd_2, "c", 1)
    ahead = add(after(ahead, grads[0], back), mine[3])
    grads = grads_of(
        "grads_4", ((4, (0, 1, 2, 3)),), 72, (even_0, even_2, even_0c, even_2c), grads, (ahead, odd_2)
    )
    ahead = after(shift(ahead, "z", 1), grads[0])
    send = sum_of(mine[0, 1], ahead[1], back[1])
    keep = mine[0, 0].astype(F32) + ahead[0].astype(F32) + back[0].astype(F32)
    gate_grad, up_grad = grads_of("grads_5", ((5, (0, 0, 1, 1)),), 40, (odd_2, odd_2c), grads, (send,))
    input_grad = (keep + after(shift(send, "yl", 1), gate_grad).astype(F32)).astype(BF)
    return input_grad, gate_grad, up_grad


def solution(mesh):
    fine = Mesh(mesh.devices.reshape(2, 2, 4, 4, 2), ("yh", "c", "x", "z", "yl"))
    tok, wt = ("yh", "c"), ("x", "z", "yl")
    in_specs = (P(tok, wt),) * 4 + (P(wt, None, None),) * 2 + (P(wt),) * 3
    out_specs = (P(tok, wt), P(wt, None, None), P(wt, None, None))
    return jax.shard_map(body, mesh=fine, in_specs=in_specs, out_specs=out_specs, check_vma=False)
```
